512 devices in a mesh: group: 32 (over y, x), member: 16 (over z, core).
Axes of the slice: x: 4, y: 8, z: 8, core: 2. Of those that a mesh axis runs over, the one named last changes fastest.
Arguments:
- passages: bfloat16 [524288, 768], P(('group', 'member')), may hold values from -32 to 32
- labels: int32 [524288], P(('group', 'member')), may hold values from 0 to 127
- send_counts: int32 [512, 32], P(('group', 'member')), may hold values from 24 to 40, as said below
- send_offsets: int32 [512, 32], P(('group', 'member')), may hold values from 0 to 1024, as said below
- owner_slot: int32 [128], replicated, may hold values from 0 to 127, as said below
- centroids: bfloat16 [12800, 768], P(('group', 'member')), may hold values from -2 to 2
Outputs:
- new_centroids: float32 [12800, 768], P(('group', 'member'))
The draws below stay inside these ranges and needn't reach their ends.
Inputs may be any that keep to these rules, and one draw needn't show every extreme that they name: On each device, rows send_offsets[g] to send_offsets[g] + send_counts[g] - 1 hold the passages whose cluster is owned by group g, that is owner_slot[label] // 4 = g. `send_counts`: A device sends at most 40 passages to one group, and its counts sum to 1024; in every draw some group receives 40 from every device. A permutation of the slots; cluster c is owned by group owner_slot[c] // 4.
All inputs are finite; a program needn't handle non-finite values.
Results may differ from the reference program's by a relative error of at most 0.003.
Values may be sent and summed in bfloat16 or wider, within the bound.
No kernel may reach another device: no remote copies, remote signals or barrier semaphores. Data moves between devices by JAX's collectives and lax.ppermute only.
A program may use at most 64 MiB of HBM per device.

```python
import math
import jax
import jax.numpy as jnp
from jax import lax

D = 768
K = 100
CL_GRP = 4
ITERS = 2
ROWS_DEV = 1024
CAP = 40
CLUSTERS = 128
PASSAGES = 524288
N_GROUP = 32
DEVICES = 512


def route_tables(key):
    slot_table = jax.random.permutation(jax.random.fold_in(key, 101), CLUSTERS).astype(jnp.int32)
    pairing = jax.random.permutation(jax.random.fold_in(key, 102), N_GROUP).astype(jnp.int32)
    half_groups = N_GROUP // 2
    mean_load = ROWS_DEV // N_GROUP
    spread = CAP - mean_load
    first_draw = jax.random.randint(jax.random.fold_in(key, 103), (DEVICES, half_groups), 0, spread + 1, dtype=jnp.int32)
    second_draw = jax.random.randint(jax.random.fold_in(key, 104), (DEVICES, half_groups), 0, spread + 1, dtype=jnp.int32)
    upper_load = mean_load + jnp.maximum(first_draw, second_draw)
    upper_load = upper_load.at[:, 0].set(CAP)
    counts = jnp.zeros((DEVICES, N_GROUP), jnp.int32)
    counts = counts.at[:, pairing[0::2]].set(upper_load)
    counts = counts.at[:, pairing[1::2]].set(2 * mean_load - upper_load)
    end_rows = jnp.cumsum(counts, axis=1).astype(jnp.int32)
    offsets = (end_rows - counts).astype(jnp.int32)
    positions = jnp.arange(ROWS_DEV, dtype=jnp.int32)
    destination = jax.vmap(lambda end_row: jnp.searchsorted(end_row, positions, side='right'))(end_rows).astype(jnp.int32)
    cluster_of_slot = jnp.zeros((CLUSTERS,), jnp.int32).at[slot_table].set(jnp.arange(CLUSTERS, dtype=jnp.int32))
    chosen = jax.random.randint(jax.random.fold_in(key, 105), (DEVICES, ROWS_DEV), 0, CL_GRP, dtype=jnp.int32)
    labels = cluster_of_slot[destination * CL_GRP + chosen]
    return (slot_table, counts, offsets, labels.reshape(PASSAGES).astype(jnp.int32))


def centroid_table(key):
    values = jax.random.normal(jax.random.fold_in(key, 106), (CLUSTERS * K, D), jnp.float32)
    return 0.5 * jnp.clip(values, -4.0, 4.0)


def draw_passages(key, part):
    key = jax.random.fold_in(key, 7)
    values = jnp.clip(jax.random.normal(jax.random.fold_in(key, 5), (PASSAGES, D), jnp.float32), -6.0, 6.0)
    return values.astype(jnp.bfloat16)


def draw_labels(key, part):
    return route_tables(key)[3]


def draw_send_counts(key, part):
    return route_tables(key)[1]


def draw_send_offsets(key, part):
    return route_tables(key)[2]


def draw_owner_slot(key, part):
    return route_tables(key)[0]


def draw_centroids(key, part):
    return centroid_table(key).astype(jnp.bfloat16)


def setup_inputs(seed: int = 0) -> dict:
    streams_of = jax.random.split(jax.random.key(seed), 7)
    return {
        "passages": draw_passages(jax.random.fold_in(streams_of[6], 71), 0),
        "labels": draw_labels(jax.random.fold_in(streams_of[6], 71), 0),
        "send_counts": draw_send_counts(jax.random.fold_in(streams_of[6], 71), 0),
        "send_offsets": draw_send_offsets(jax.random.fold_in(streams_of[6], 71), 0),
        "owner_slot": draw_owner_slot(jax.random.fold_in(streams_of[6], 71), 0),
        "centroids": draw_centroids(jax.random.fold_in(streams_of[6], 71), 0),
    }


temper = 16.0


def reference(passages, labels, send_counts, send_offsets, owner_slot, centroids):
    local_slot = (owner_slot[labels] % CL_GRP).astype(jnp.int32).reshape(DEVICES, ROWS_DEV)
    slot_index = jnp.arange(CAP, dtype=jnp.int32)[None, None, :]
    usable = slot_index < send_counts[:, :, None]
    source_rows = jnp.where(usable, jnp.minimum(send_offsets[:, :, None] + slot_index, ROWS_DEV - 1), 0).astype(jnp.int32)
    device_index = jnp.arange(DEVICES, dtype=jnp.int32)[:, None, None]
    group_index = jnp.arange(N_GROUP, dtype=jnp.int32)[None, :, None]
    global_rows = (device_index * ROWS_DEV + source_rows).astype(jnp.int32)
    slot = (group_index * CL_GRP + local_slot[device_index, source_rows]).astype(jnp.int32)
    live = usable.astype(jnp.float32)
    items = DEVICES * N_GROUP * CAP
    block_rows = math.gcd(items, 128)
    row_blocks = global_rows.reshape(-1, block_rows)
    slot_blocks = slot.reshape(-1, block_rows)
    live_blocks = live.reshape(-1, block_rows)
    current = centroids.astype(jnp.float32).reshape(CLUSTERS, K, D)
    for sweep in range(ITERS):
        rounded = lax.optimization_barrier(current.astype(jnp.bfloat16)).astype(jnp.float32)
        lengths = jnp.sum(rounded * rounded, axis=-1)

        def accumulate(totals_pair, item_triple):
            numerator, totals = totals_pair
            row_ids, slot_block, live_block = item_triple
            row_float = passages[row_ids].astype(jnp.float32)
            nearby = rounded[slot_block]
            inner = jnp.einsum('rd,rkd->rk', row_float, nearby)
            logits = (2.0 * inner - lengths[slot_block]) / temper
            highest = jnp.max(logits, axis=1, keepdims=True)
            exponent = jnp.exp(logits - highest)
            weights = exponent / jnp.sum(exponent, axis=1, keepdims=True) * live_block[:, None]
            totals = totals.at[slot_block].add(weights)
            weight_bf = lax.optimization_barrier(weights.astype(jnp.bfloat16)).astype(jnp.float32)
            numerator = numerator.at[slot_block].add(jnp.einsum('rk,rd->rkd', weight_bf, row_float))
            return (numerator, totals), None

        start = (jnp.zeros((CLUSTERS, K, D), jnp.float32), jnp.zeros((CLUSTERS, K), jnp.float32))
        (numerator, totals), unused = lax.scan(accumulate, start, (row_blocks, slot_blocks, live_blocks))
        current = (numerator + current) / (totals[..., None] + 1.0)
    return current.reshape(CLUSTERS * K, D)
```

```python
import functools

import jax
import jax.numpy as jnp
from jax import lax
from jax.experimental import pallas as pl
from jax.experimental.pallas import tpu as pltpu
from jax.sharding import PartitionSpec as P

K = 100
CL_GRP = 4
ITERS = 2
temper = 16.0

GROUPS = 32
CAP = 40
WINDOW = CAP + 8
HEAD = 32
LANES = 128
CHUNKS = 6
SEND_ROWS = 256
ZS = 8
OWN = 25
BLOCK = 32
PACK = 160
HALF = ZS * BLOCK
ITEMS = GROUPS * CAP
STEP = 256
f32 = jnp.float32
bf16 = jnp.bfloat16

ON_CHIP = pl.BlockSpec(memory_space=pltpu.VMEM)
SCALARS = pl.BlockSpec(memory_space=pltpu.SMEM)


def iota(shape, axis):
    return lax.broadcasted_iota(jnp.int32, shape, axis)


def chunk(i):
    return slice(i * LANES, (i + 1) * LANES)


def to_column(row, rows):
    shape = (rows, LANES)
    return jnp.sum(jnp.where(iota(shape, 0) == iota(shape, 1), row, 0.0), axis=1, keepdims=True)


def to_row(column):
    shape = (column.shape[0], LANES)
    return jnp.sum(jnp.where(iota(shape, 0) == iota(shape, 1), column, 0.0), axis=0, keepdims=True)


def front_kernel(counts, offsets, me, labels, owner, rows, out, wide, tags):
    local = jnp.bitwise_and(owner[...], CL_GRP - 1).astype(f32) + 1.0
    local = to_column(local, LANES)
    square = (LANES, LANES)
    for q in range(labels.shape[0]):
        hit = jnp.where(iota(square, 0) == labels[q : q + 1, :], local, 0.0)
        column = to_column(jnp.sum(hit, axis=0, keepdims=True), LANES)
        tags[q * LANES : (q + 1) * LANES, :] = jnp.broadcast_to(column, square)
    total = rows.shape[0]
    tags[total:, :] = jnp.zeros_like(tags[total:, :])
    wide[:total, :] = rows[...].astype(f32)
    wide[total:, :] = jnp.zeros_like(wide[total:, :])
    head_base = jnp.bitwise_and(me[0], 3) * HEAD
    tail_base = jnp.bitwise_and(me[0], 15) * (CAP - HEAD)

    def one(g, carry):
        first = offsets[0, g]
        count = counts[0, g]
        window = pl.ds(pl.multiple_of(first - jnp.bitwise_and(first, 7), 8), WINDOW)
        back = WINDOW - jnp.bitwise_and(first, 7)
        picked = pltpu.roll(wide[window, :], back, 0)[:CAP]
        picked = jnp.where(iota((CAP, 1), 0) < count, picked, 0.0)
        for i in range(CHUNKS):
            out[g, i * HEAD : (i + 1) * HEAD, :] = picked[:HEAD, chunk(i)].astype(bf16)
        for q in range(CHUNKS // 2):
            both = jnp.concatenate([picked[HEAD:, chunk(2 * q)], picked[HEAD:, chunk(2 * q + 1)]], axis=0)
            start = CHUNKS * HEAD + 16 * q
            out[g, start : start + 16, :] = both.astype(bf16)
        tag = pltpu.roll(tags[window, :], back, 0)[:CAP]
        sub, lane = iota((CAP, LANES), 0), iota((CAP, LANES), 1)
        place = jnp.where(sub < HEAD, sub + head_base, sub - HEAD + tail_base)
        tag = jnp.where((lane == place) & (sub < count), tag, 0.0)
        head = jnp.sum(tag[:HEAD], axis=0, keepdims=True)
        tail = jnp.sum(tag[HEAD:], axis=0, keepdims=True)
        which = iota((16, LANES), 0)
        tile = jnp.where(which == 0, head, jnp.where(which == 1, tail, 0.0))
        out[g, SEND_ROWS - 16 :, :] = tile.astype(bf16)
        return carry

    lax.fori_loop(0, GROUPS, one, 0, unroll=4)


def front(counts, offsets, me, labels, owner, rows):
    spare = rows.shape[0] + WINDOW
    return pl.pallas_call(
        front_kernel,
        out_shape=jax.ShapeDtypeStruct((GROUPS, SEND_ROWS, LANES), bf16),
        in_specs=[SCALARS, SCALARS, SCALARS, ON_CHIP, ON_CHIP, ON_CHIP],
        out_specs=ON_CHIP,
        scratch_shapes=[pltpu.VMEM((spare, rows.shape[1]), f32), pltpu.VMEM((spare, LANES), f32)],
        compiler_params=pltpu.CompilerParams(vmem_limit_bytes=24 * 2**20),
        name="front",
    )(counts, offsets, me, labels.reshape(-1, LANES), owner.reshape(1, -1), rows)


def pack_rows(pieces, lasts):
    parts = [jnp.concatenate([pieces[2 * q], pieces[2 * q + 1]], axis=0) for q in range(CHUNKS // 2)]
    which = iota((16, LANES), 0)
    end = jnp.zeros((16, LANES), f32)
    for i in range(CHUNKS):
        end = jnp.where(which == i, lasts[i], end)
    return parts, end


def pack_kernel(rows, out):
    wide = rows[...].astype(f32)
    pieces = [wide[:24, chunk(i)] for i in range(CHUNKS)]
    lasts = [wide[24:25, chunk(i)] for i in range(CHUNKS)]
    parts, end = pack_rows(pieces, lasts)
    for q in range(CHUNKS // 2):
        out[0, 48 * q : 48 * q + 48, :] = parts[q].astype(bf16)
    out[0, 144:, :] = end.astype(bf16)


def pack(rows):
    return pl.pallas_call(
        pack_kernel,
        out_shape=jax.ShapeDtypeStruct((1, PACK, LANES), bf16),
        in_specs=[ON_CHIP],
        out_specs=ON_CHIP,
        compiler_params=pltpu.CompilerParams(vmem_limit_bytes=4 * 2**20),
        name="pack",
    )(rows)


def sweep_kernel(arrived, mine, theirs, send, keep, items, panel, weights, sums):
    def head(s, carry):
        for i in range(CHUNKS):
            items[pl.ds(pl.multiple_of(s * HEAD, HEAD), HEAD), chunk(i)] = arrived[s, i * HEAD : (i + 1) * HEAD, :]
        return carry

    lax.fori_loop(0, GROUPS, head, 0, unroll=4)

    def tail(u, carry):
        rows = pl.ds(pl.multiple_of(GROUPS * HEAD + 16 * u, 16), 16)
        for q in range(CHUNKS // 2):
            start = CHUNKS * HEAD + 16 * q
            even = arrived[2 * u, start : start + 16, :].astype(f32)
            odd = arrived[2 * u + 1, start : start + 16, :].astype(f32)
            items[rows, chunk(2 * q)] = jnp.concatenate([even[:8], odd[:8]], axis=0).astype(bf16)
            items[rows, chunk(2 * q + 1)] = jnp.concatenate([even[8:], odd[8:]], axis=0).astype(bf16)
        return carry

    lax.fori_loop(0, GROUPS // 2, tail, 0, unroll=4)

    def tag_tile(s):
        return arrived[s, SEND_ROWS - 16 :, :].astype(f32)[:8]

    pieces = []
    for u in range(GROUPS // 4):
        tile = sum(tag_tile(4 * u + i) for i in range(4))
        pieces.append(tile[0:1])
    for v in range(GROUPS // 16):
        tile = sum(tag_tile(16 * v + i) for i in range(16))
        pieces.append(tile[1:2])
    tags = jnp.concatenate(pieces, axis=1) - 1.0

    lengths = []
    for half, source in enumerate((mine, theirs)):
        for z in range(ZS):
            start = half * HALF + z * BLOCK
            end = source[z, 144:, :].astype(f32)[:8]
            square = jnp.zeros((BLOCK, LANES), f32)
            for q in range(CHUNKS // 2):
                part = source[z, 48 * q : 48 * q + 48, :].astype(f32)
                for i in (2 * q, 2 * q + 1):
                    low = 24 * (i % 2)
                    last = jnp.where(iota((8, LANES), 0) == 0, end[i : i + 1], 0.0)
                    piece = jnp.concatenate([part[low : low + 24], last], axis=0)
                    square = square + piece * piece
                    panel[start : start + BLOCK, chunk(i)] = piece.astype(bf16)
            lengths.append(jnp.sum(square, axis=1, keepdims=True))
    lengths = jnp.concatenate(lengths, axis=0) * (1.0 / temper)

    part_rows = HALF // CL_GRP
    real = (iota((part_rows, 1), 0) % BLOCK) < OWN
    totals = [jnp.zeros((part_rows, LANES), f32) for _ in range(2 * CL_GRP)]
    for j in range(ITEMS // STEP):
        columns = slice(j * STEP, (j + 1) * STEP)
        product = lax.dot_general(
            panel[...], items[columns, :], (((1,), (1,)), ((), ())), preferred_element_type=f32
        )
        logits = product * (2.0 / temper) - lengths
        tag = tags[:, columns]
        picked = []
        for half in range(2):
            rows = [
                logits[half * HALF + c * part_rows : half * HALF + (c + 1) * part_rows]
                for c in range(CL_GRP)
            ]
            chosen = rows[0]
            for c in range(1, CL_GRP):
                chosen = jnp.where(tag == c, rows[c], chosen)
            picked.append(jnp.where(real, chosen, -3e38))
        highest = jnp.maximum(
            jnp.max(picked[0], axis=0, keepdims=True), jnp.max(picked[1], axis=0, keepdims=True)
        )
        exponent = [jnp.exp(p - highest) for p in picked]
        scale = 1.0 / (
            jnp.sum(exponent[0], axis=0, keepdims=True) + jnp.sum(exponent[1], axis=0, keepdims=True)
        )
        for half in range(2):
            weight = exponent[half] * scale
            for c in range(CL_GRP):
                own = jnp.where(tag == c, weight, 0.0)
                start = half * HALF + c * part_rows
                weights[start : start + part_rows, columns] = own.astype(bf16)
                n = half * CL_GRP + c
                for i in range(STEP // LANES):
                    totals[n] = totals[n] + own[:, chunk(i)]

    for half, out in ((1, send), (0, keep)):
        sums[...] = jnp.dot(
            weights[half * HALF : (half + 1) * HALF, :], items[...], preferred_element_type=f32
        )
        for z in range(ZS):
            start = z * BLOCK
            end = jnp.zeros((8, LANES), f32)
            for i in range(CHUNKS):
                out[z, 24 * i : 24 * i + 24, :] = sums[start : start + 24, chunk(i)]
                end = jnp.where(iota((8, LANES), 0) == i, sums[start + 24 : start + 25, chunk(i)], end)
            block = totals[half * CL_GRP + z // 2][(z % 2) * BLOCK : (z % 2 + 1) * BLOCK]
            total = to_row(jnp.sum(block, axis=1, keepdims=True))
            out[z, 144:152, :] = jnp.where(iota((8, LANES), 0) == 6, total, end)
            out[z, 152:, :] = jnp.zeros((8, LANES), f32)


def sweep(arrived, mine, theirs):
    shape = jax.ShapeDtypeStruct((ZS, PACK, LANES), f32)
    return pl.pallas_call(
        sweep_kernel,
        out_shape=(shape, shape),
        in_specs=[ON_CHIP] * 3,
        out_specs=(ON_CHIP, ON_CHIP),
        scratch_shapes=[
            pltpu.VMEM((ITEMS, CHUNKS * LANES), bf16),
            pltpu.VMEM((2 * HALF, CHUNKS * LANES), bf16),
            pltpu.VMEM((2 * HALF, ITEMS), bf16),
            pltpu.VMEM((HALF, CHUNKS * LANES), f32),
        ],
        compiler_params=pltpu.CompilerParams(vmem_limit_bytes=32 * 2**20),
        name="sweep",
    )(arrived, mine, theirs)


def join_kernel(keep, received, out):
    which = iota((8, LANES), 0)
    for z in range(ZS):
        out[z, :144, :] = (keep[z, :144, :] + received[z, :144, :]).astype(bf16)
        end = keep[z, 144:152, :] + received[z, 144:152, :]
        rest = end - end.astype(bf16).astype(f32)
        end = jnp.where(which == 7, rest[6:7], end)
        out[z, 144:, :] = jnp.concatenate([end, jnp.zeros_like(end)], axis=0).astype(bf16)


def join(keep, received):
    return pl.pallas_call(
        join_kernel,
        out_shape=jax.ShapeDtypeStruct((ZS, PACK, LANES), bf16),
        in_specs=[ON_CHIP] * 2,
        out_specs=ON_CHIP,
        compiler_params=pltpu.CompilerParams(vmem_limit_bytes=8 * 2**20),
        name="join",
    )(keep, received)


def update_kernel(parts, prior, out, *copies):
    total = parts[0].astype(f32)
    for z in range(1, ZS):
        total = total + parts[z].astype(f32)
    end = total[144:152]
    weight = to_column(end[6:7] + end[7:8], BLOCK) + 1.0
    before = prior[...].astype(f32)
    pieces, lasts = [], []
    for i in range(CHUNKS):
        piece = (total[24 * i : 24 * i + 24] + before[:24, chunk(i)]) / weight[:24]
        last = (end[i : i + 1] + before[24:25, chunk(i)]) / weight[24:25]
        out[:24, chunk(i)] = piece
        out[24:25, chunk(i)] = last
        pieces.append(piece)
        lasts.append(last)
    if copies:
        parts, end = pack_rows(pieces, lasts)
        parts = [p.astype(bf16) for p in parts]
        end = end.astype(bf16)
        for z in range(ZS):
            for q in range(CHUNKS // 2):
                copies[0][z, 48 * q : 48 * q + 48, :] = parts[q]
            copies[0][z, 144:, :] = end


def update(parts, prior, last):
    out_shape = [jax.ShapeDtypeStruct((OWN, CHUNKS * LANES), f32)]
    if not last:
        out_shape.append(jax.ShapeDtypeStruct((ZS, PACK, LANES), bf16))
    return pl.pallas_call(
        update_kernel,
        out_shape=out_shape,
        in_specs=[ON_CHIP] * 2,
        out_specs=[ON_CHIP] * len(out_shape),
        compiler_params=pltpu.CompilerParams(vmem_limit_bytes=8 * 2**20),
        name="update",
    )(parts, prior)


def shards(passages, labels, send_counts, send_offsets, owner_slot, centroids):
    members = lax.axis_size("member")
    along_z = [[m for m in range(members) if m % 2 == core] for core in range(2)]
    cores = [(m, m ^ 1) for m in range(members)]
    me = lax.axis_index("group").reshape(1).astype(jnp.int32)

    outgoing = front(send_counts, send_offsets, me, labels, owner_slot, passages)
    arrived = lax.all_to_all(outgoing, "group", split_axis=0, concat_axis=0, tiled=True)
    mine = lax.all_gather(pack(centroids), "member", axis=0, tiled=True, axis_index_groups=along_z)
    theirs = lax.ppermute(mine, "member", cores)
    prior = centroids
    for turn in range(ITERS):
        send, keep = sweep(arrived, mine, theirs)
        received = lax.ppermute(send, "member", cores)
        parts = lax.all_to_all(
            join(keep, received), "member", split_axis=0, concat_axis=0, tiled=True, axis_index_groups=along_z
        )
        last = turn == ITERS - 1
        prior, *copies = update(parts, prior, last)
        if not last:
            mine = lax.all_to_all(
                copies[0], "member", split_axis=0, concat_axis=0, tiled=True, axis_index_groups=along_z
            )
            theirs = lax.ppermute(mine, "member", cores)
    return prior


def solution(mesh):
    spec = P(("group", "member"))
    rows = P(("group", "member"), None)
    return jax.shard_map(
        shards,
        mesh=mesh,
        in_specs=(rows, spec, rows, rows, P(), rows),
        out_specs=rows,
        check_vma=False,
    )
```

```python
import functools

import jax
import jax.numpy as jnp
from jax import lax
from jax.experimental import pallas as pl
from jax.experimental.pallas import tpu as pltpu
from jax.sharding import PartitionSpec as P

K = 100
CL_GRP = 4
ITERS = 2
temper = 16.0

GROUPS = 32
CAP = 40
WINDOW = CAP + 8
HEAD = 32
LANES = 128
CHUNKS = 6
TAG_ROWS = 8
SEND_ROWS = 240 + TAG_ROWS
ROW_PARTS = 4
OUT_PARTS = 4
ZS = 8
OWN = 25
BLOCK = 32
PACK = 152
HALF = ZS * BLOCK
ITEMS = GROUPS * CAP
STEP = 256
f32 = jnp.float32
bf16 = jnp.bfloat16

ON_CHIP = pl.BlockSpec(memory_space=pltpu.VMEM)
FAR = pl.BlockSpec(memory_space=pltpu.HBM)
SCALARS = pl.BlockSpec(memory_space=pltpu.SMEM)


def iota(shape, axis):
    return lax.broadcasted_iota(jnp.int32, shape, axis)


def chunk(i):
    return slice(i * LANES, (i + 1) * LANES)


def to_column(row, rows):
    shape = (rows, LANES)
    return jnp.sum(jnp.where(iota(shape, 0) == iota(shape, 1), row, 0.0), axis=1, keepdims=True)


def to_row(column):
    shape = (column.shape[0], LANES)
    return jnp.sum(jnp.where(iota(shape, 0) == iota(shape, 1), column, 0.0), axis=0, keepdims=True)


def front_kernel(me, counts_in, offsets_in, labels_in, owner_in, rows_in, out_far, *scratch):
    counts, offsets, labels, owner, rows, wide, tags, out, small_done, rows_done, out_done = scratch
    total = rows.shape[0]
    part = total // ROW_PARTS
    small = [
        pltpu.make_async_copy(source, target, small_done.at[i])
        for i, (source, target) in enumerate(
            ((labels_in, labels), (owner_in, owner), (counts_in, counts), (offsets_in, offsets))
        )
    ]
    for copy in small:
        copy.start()
    parts = []
    for i in range(ROW_PARTS):
        where = pl.ds(i * part, part)
        parts.append(pltpu.make_async_copy(rows_in.at[where], rows.at[where], rows_done.at[i]))
        parts[-1].start()
    tags[total:, :] = jnp.zeros_like(tags[total:, :])
    wide[total:, :] = jnp.zeros_like(wide[total:, :])
    small[0].wait()
    small[1].wait()
    local = jnp.bitwise_and(owner[...], CL_GRP - 1).astype(f32) + 1.0
    local = to_column(local, LANES)
    square = (LANES, LANES)
    for q in range(labels.shape[0]):
        hit = jnp.where(iota(square, 0) == labels[q : q + 1, :], local, 0.0)
        column = to_column(jnp.sum(hit, axis=0, keepdims=True), LANES)
        tags[q * LANES : (q + 1) * LANES, :] = jnp.broadcast_to(column, square)
    for i in range(ROW_PARTS):
        parts[i].wait()
        wide[i * part : (i + 1) * part, :] = rows[i * part : (i + 1) * part, :].astype(f32)
    small[2].wait()
    small[3].wait()
    head_base = jnp.bitwise_and(me[0], 3) * HEAD
    tail_base = jnp.bitwise_and(me[0], 15) * (CAP - HEAD)

    def one(g, carry):
        first = offsets[0, g]
        count = counts[0, g]
        window = pl.ds(pl.multiple_of(first - jnp.bitwise_and(first, 7), 8), WINDOW)
        back = WINDOW - jnp.bitwise_and(first, 7)
        picked = pltpu.roll(wide[window, :], back, 0)[:CAP]
        picked = jnp.where(iota((CAP, 1), 0) < count, picked, 0.0)
        for i in range(CHUNKS):
            out[g, i * HEAD : (i + 1) * HEAD, :] = picked[:HEAD, chunk(i)].astype(bf16)
        for q in range(CHUNKS // 2):
            both = jnp.concatenate([picked[HEAD:, chunk(2 * q)], picked[HEAD:, chunk(2 * q + 1)]], axis=0)
            start = CHUNKS * HEAD + 16 * q
            out[g, start : start + 16, :] = both.astype(bf16)
        tag = pltpu.roll(tags[window, :], back, 0)[:CAP]
        sub, lane = iota((CAP, LANES), 0), iota((CAP, LANES), 1)
        place = jnp.where(sub < HEAD, sub + head_base, sub - HEAD + tail_base)
        tag = jnp.where((lane == place) & (sub < count), tag, 0.0)
        head = jnp.sum(tag[:HEAD], axis=0, keepdims=True)
        tail = jnp.sum(tag[HEAD:], axis=0, keepdims=True)
        which = iota((TAG_ROWS, LANES), 0)
        tile = jnp.where(which == 0, head, jnp.where(which == 1, tail, 0.0))
        out[g, SEND_ROWS - TAG_ROWS :, :] = tile.astype(bf16)
        return carry

    batch = GROUPS // OUT_PARTS
    sent = []
    for i in range(OUT_PARTS):
        lax.fori_loop(i * batch, (i + 1) * batch, one, 0, unroll=4)
        where = pl.ds(i * batch, batch)
        sent.append(pltpu.make_async_copy(out.at[where], out_far.at[where], out_done.at[i]))
        sent[-1].start()
    for copy in sent:
        copy.wait()


def front(me, counts, offsets, labels, owner, rows):
    spare = rows.shape[0] + WINDOW
    labels = labels.reshape(-1, LANES)
    owner = owner.reshape(1, -1)
    sent = (GROUPS, SEND_ROWS, LANES)
    return pl.pallas_call(
        front_kernel,
        out_shape=jax.ShapeDtypeStruct(sent, bf16),
        in_specs=[SCALARS] + [FAR] * 5,
        out_specs=FAR,
        scratch_shapes=[
            pltpu.SMEM(counts.shape, jnp.int32),
            pltpu.SMEM(offsets.shape, jnp.int32),
            pltpu.VMEM(labels.shape, jnp.int32),
            pltpu.VMEM(owner.shape, jnp.int32),
            pltpu.VMEM(rows.shape, bf16),
            pltpu.VMEM((spare, rows.shape[1]), f32),
            pltpu.VMEM((spare, LANES), f32),
            pltpu.VMEM(sent, bf16),
            pltpu.SemaphoreType.DMA((4,)),
            pltpu.SemaphoreType.DMA((ROW_PARTS,)),
            pltpu.SemaphoreType.DMA((OUT_PARTS,)),
        ],
        name="front",
    )(me, counts, offsets, labels, owner, rows)


def pack_rows(pieces, lasts):
    parts = [jnp.concatenate([pieces[2 * q], pieces[2 * q + 1]], axis=0) for q in range(CHUNKS // 2)]
    which = iota((8, LANES), 0)
    end = jnp.zeros((8, LANES), f32)
    for i in range(CHUNKS):
        end = jnp.where(which == i, lasts[i], end)
    return parts, end


def pack_kernel(rows, out):
    wide = rows[...].astype(f32)
    pieces = [wide[:24, chunk(i)] for i in range(CHUNKS)]
    lasts = [wide[24:25, chunk(i)] for i in range(CHUNKS)]
    parts, end = pack_rows(pieces, lasts)
    for q in range(CHUNKS // 2):
        out[0, 48 * q : 48 * q + 48, :] = parts[q].astype(bf16)
    out[0, 144:, :] = end.astype(bf16)


def pack(rows):
    return pl.pallas_call(
        pack_kernel,
        out_shape=jax.ShapeDtypeStruct((1, PACK, LANES), bf16),
        in_specs=[ON_CHIP],
        out_specs=ON_CHIP,
        compiler_params=pltpu.CompilerParams(vmem_limit_bytes=4 * 2**20),
        name="pack",
    )(rows)


def unpack_items(arrived, items, tags):
    def head(s, carry):
        for i in range(CHUNKS):
            items[pl.ds(pl.multiple_of(s * HEAD, HEAD), HEAD), chunk(i)] = arrived[s, i * HEAD : (i + 1) * HEAD, :]
        return carry

    lax.fori_loop(0, GROUPS, head, 0, unroll=4)

    def tail(u, carry):
        rows = pl.ds(pl.multiple_of(GROUPS * HEAD + 16 * u, 16), 16)
        for q in range(CHUNKS // 2):
            start = CHUNKS * HEAD + 16 * q
            even = arrived[2 * u, start : start + 16, :].astype(f32)
            odd = arrived[2 * u + 1, start : start + 16, :].astype(f32)
            items[rows, chunk(2 * q)] = jnp.concatenate([even[:8], odd[:8]], axis=0).astype(bf16)
            items[rows, chunk(2 * q + 1)] = jnp.concatenate([even[8:], odd[8:]], axis=0).astype(bf16)
        return carry

    lax.fori_loop(0, GROUPS // 2, tail, 0, unroll=4)

    def tag_tile(s):
        return arrived[s, SEND_ROWS - TAG_ROWS :, :].astype(f32)

    pieces = []
    for u in range(GROUPS // 4):
        tile = sum(tag_tile(4 * u + i) for i in range(4))
        pieces.append(tile[0:1])
    for v in range(GROUPS // 16):
        tile = sum(tag_tile(16 * v + i) for i in range(16))
        pieces.append(tile[1:2])
    tags[...] = jnp.concatenate(pieces, axis=1) - 1.0


def sweep_kernel(first, core, *refs):
    if first:
        arrived, blocks, send, keep, items, tags, panel, weights, sums = refs
        unpack_items(arrived, items, tags)
    else:
        items, tags, blocks, send, keep, panel, weights, sums = refs

    lengths = []
    for half in range(2):
        for z in range(ZS):
            start = half * HALF + z * BLOCK
            source = 2 * z + jnp.bitwise_xor(core[0], half)
            end = blocks[source, 144:, :].astype(f32)
            square = jnp.zeros((BLOCK, LANES), f32)
            for q in range(CHUNKS // 2):
                part = blocks[source, 48 * q : 48 * q + 48, :].astype(f32)
                for i in (2 * q, 2 * q + 1):
                    low = 24 * (i % 2)
                    last = jnp.where(iota((8, LANES), 0) == 0, end[i : i + 1], 0.0)
                    piece = jnp.concatenate([part[low : low + 24], last], axis=0)
                    square = square + piece * piece
                    panel[start : start + BLOCK, chunk(i)] = piece.astype(bf16)
            lengths.append(jnp.sum(square, axis=1, keepdims=True))
    lengths = jnp.concatenate(lengths, axis=0) * (1.0 / temper)

    part_rows = HALF // CL_GRP
    real = (iota((part_rows, 1), 0) % BLOCK) < OWN
    totals = [jnp.zeros((part_rows, LANES), f32) for _ in range(2 * CL_GRP)]
    for j in range(ITEMS // STEP):
        columns = slice(j * STEP, (j + 1) * STEP)
        product = lax.dot_general(
            panel[...], items[columns, :], (((1,), (1,)), ((), ())), preferred_element_type=f32
        )
        logits = product * (2.0 / temper) - lengths
        tag = tags[:, columns]
        picked = []
        for half in range(2):
            rows = [
                logits[half * HALF + c * part_rows : half * HALF + (c + 1) * part_rows]
                for c in range(CL_GRP)
            ]
            chosen = rows[0]
            for c in range(1, CL_GRP):
                chosen = jnp.where(tag == c, rows[c], chosen)
            picked.append(jnp.where(real, chosen, -3e38))
        highest = jnp.maximum(
            jnp.max(picked[0], axis=0, keepdims=True), jnp.max(picked[1], axis=0, keepdims=True)
        )
        exponent = [jnp.exp(p - highest) for p in picked]
        scale = 1.0 / (
            jnp.sum(exponent[0], axis=0, keepdims=True) + jnp.sum(exponent[1], axis=0, keepdims=True)
        )
        for half in range(2):
            weight = exponent[half] * scale
            for c in range(CL_GRP):
                own = jnp.where(tag == c, weight, 0.0)
                start = half * HALF + c * part_rows
                weights[start : start + part_rows, columns] = own.astype(bf16)
                n = half * CL_GRP + c
                for i in range(STEP // LANES):
                    totals[n] = totals[n] + own[:, chunk(i)]

    for half, out in ((1, send), (0, keep)):
        sums[...] = jnp.dot(
            weights[half * HALF : (half + 1) * HALF, :], items[...], preferred_element_type=f32
        )
        for z in range(ZS):
            start = z * BLOCK
            end = jnp.zeros((8, LANES), f32)
            for i in range(CHUNKS):
                out[z, 24 * i : 24 * i + 24, :] = sums[start : start + 24, chunk(i)]
                end = jnp.where(iota((8, LANES), 0) == i, sums[start + 24 : start + 25, chunk(i)], end)
            block = totals[half * CL_GRP + z // 2][(z % 2) * BLOCK : (z % 2 + 1) * BLOCK]
            total = to_row(jnp.sum(block, axis=1, keepdims=True))
            out[z, 144:152, :] = jnp.where(iota((8, LANES), 0) == 6, total, end)


def sweep(core, passages, blocks, first):
    sums = jax.ShapeDtypeStruct((ZS, PACK, LANES), f32)
    out_shape = [sums, sums]
    if first:
        out_shape.append(jax.ShapeDtypeStruct((ITEMS, CHUNKS * LANES), bf16))
        out_shape.append(jax.ShapeDtypeStruct((1, ITEMS), f32))
    return pl.pallas_call(
        functools.partial(sweep_kernel, first),
        out_shape=out_shape,
        in_specs=[SCALARS] + [ON_CHIP] * (len(passages) + 1),
        out_specs=[ON_CHIP] * len(out_shape),
        scratch_shapes=[
            pltpu.VMEM((2 * HALF, CHUNKS * LANES), bf16),
            pltpu.VMEM((2 * HALF, ITEMS), bf16),
            pltpu.VMEM((HALF, CHUNKS * LANES), f32),
        ],
        compiler_params=pltpu.CompilerParams(vmem_limit_bytes=32 * 2**20),
        name="sweep",
    )(core, *passages, blocks)


def join_kernel(keep, received, out):
    which = iota((8, LANES), 0)
    for z in range(ZS):
        out[z, :144, :] = (keep[z, :144, :] + received[z, :144, :]).astype(bf16)
        end = keep[z, 144:152, :] + received[z, 144:152, :]
        rest = end - end.astype(bf16).astype(f32)
        end = jnp.where(which == 7, rest[6:7], end)
        out[z, 144:, :] = end.astype(bf16)


def join(keep, received):
    return pl.pallas_call(
        join_kernel,
        out_shape=jax.ShapeDtypeStruct((ZS, PACK, LANES), bf16),
        in_specs=[ON_CHIP] * 2,
        out_specs=ON_CHIP,
        compiler_params=pltpu.CompilerParams(vmem_limit_bytes=8 * 2**20),
        name="join",
    )(keep, received)


def update_kernel(parts, prior, out, *packed):
    total = parts[0].astype(f32)
    for z in range(1, ZS):
        total = total + parts[z].astype(f32)
    end = total[144:152]
    weight = to_column(end[6:7] + end[7:8], BLOCK) + 1.0
    before = prior[...].astype(f32)
    pieces, lasts = [], []
    for i in range(CHUNKS):
        piece = (total[24 * i : 24 * i + 24] + before[:24, chunk(i)]) / weight[:24]
        last = (end[i : i + 1] + before[24:25, chunk(i)]) / weight[24:25]
        out[:24, chunk(i)] = piece
        out[24:25, chunk(i)] = last
        pieces.append(piece)
        lasts.append(last)
    if packed:
        parts, end = pack_rows(pieces, lasts)
        for q in range(CHUNKS // 2):
            packed[0][0, 48 * q : 48 * q + 48, :] = parts[q].astype(bf16)
        packed[0][0, 144:, :] = end.astype(bf16)


def update(parts, prior, last):
    out_shape = [jax.ShapeDtypeStruct((OWN, CHUNKS * LANES), f32)]
    if not last:
        out_shape.append(jax.ShapeDtypeStruct((1, PACK, LANES), bf16))
    return pl.pallas_call(
        update_kernel,
        out_shape=out_shape,
        in_specs=[ON_CHIP] * 2,
        out_specs=[ON_CHIP] * len(out_shape),
        compiler_params=pltpu.CompilerParams(vmem_limit_bytes=8 * 2**20),
        name="update",
    )(parts, prior)


def shards(passages, labels, send_counts, send_offsets, owner_slot, centroids):
    members = lax.axis_size("member")
    along_z = [[m for m in range(members) if m % 2 == core] for core in range(2)]
    cores = [(m, m ^ 1) for m in range(members)]
    me = lax.axis_index("group").reshape(1).astype(jnp.int32)
    core = jnp.bitwise_and(lax.axis_index("member"), 1).reshape(1).astype(jnp.int32)

    outgoing = front(me, send_counts, send_offsets, labels, owner_slot, passages)
    passage_refs = [lax.all_to_all(outgoing, "group", split_axis=0, concat_axis=0, tiled=True)]
    packed = pack(centroids)
    prior = centroids
    for turn in range(ITERS):
        blocks = lax.all_gather(packed, "member", axis=0, tiled=True)
        send, keep, *unpacked = sweep(core, passage_refs, blocks, turn == 0)
        passage_refs = unpacked or passage_refs
        received = lax.ppermute(send, "member", cores)
        parts = lax.all_to_all(
            join(keep, received), "member", split_axis=0, concat_axis=0, tiled=True, axis_index_groups=along_z
        )
        prior, *packed = update(parts, prior, turn == ITERS - 1)
        packed = packed[0] if packed else None
    return prior


def solution(mesh):
    spec = P(("group", "member"))
    rows = P(("group", "member"), None)
    return jax.shard_map(
        shards,
        mesh=mesh,
        in_specs=(rows, spec, rows, rows, P(), rows),
        out_specs=rows,
        check_vma=False,
    )
```

```python
import functools

import jax
import jax.numpy as jnp
from jax import lax
from jax.experimental import pallas as pl
from jax.experimental.pallas import tpu as pltpu
from jax.sharding import PartitionSpec as P

K = 100
CL_GRP = 4
ITERS = 2
temper = 16.0

GROUPS = 32
CAP = 40
WINDOW = CAP + 8
HEAD = 32
LANES = 128
CHUNKS = 6
TAG_ROWS = 8
SEND_ROWS = 240 + TAG_ROWS
ROW_PARTS = 4
OUT_PARTS = 4
ZS = 8
OWN = 25
BLOCK = 32
PACK = 152
MAIN = ZS * 24
LASTS = 32
PANEL = 2 * MAIN + LASTS
ITEMS = GROUPS * CAP
STEP = 256
f32 = jnp.float32
bf16 = jnp.bfloat16

ON_CHIP = pl.BlockSpec(memory_space=pltpu.VMEM)
FAR = pl.BlockSpec(memory_space=pltpu.HBM)
SCALARS = pl.BlockSpec(memory_space=pltpu.SMEM)


def iota(shape, axis):
    return lax.broadcasted_iota(jnp.int32, shape, axis)


def chunk(i):
    return slice(i * LANES, (i + 1) * LANES)


def to_column(row, rows):
    shape = (rows, LANES)
    return jnp.sum(jnp.where(iota(shape, 0) == iota(shape, 1), row, 0.0), axis=1, keepdims=True)


def to_row(column):
    shape = (column.shape[0], LANES)
    return jnp.sum(jnp.where(iota(shape, 0) == iota(shape, 1), column, 0.0), axis=0, keepdims=True)


def front_kernel(me, counts_in, offsets_in, labels_in, owner_in, rows_in, out_far, *scratch):
    counts, offsets, labels, owner, rows, wide, tags, out, small_done, rows_done, out_done = scratch
    total = rows.shape[0]
    part = total // ROW_PARTS
    small = [
        pltpu.make_async_copy(source, target, small_done.at[i])
        for i, (source, target) in enumerate(
            ((labels_in, labels), (owner_in, owner), (counts_in, counts), (offsets_in, offsets))
        )
    ]
    for copy in small:
        copy.start()
    parts = []
    for i in range(ROW_PARTS):
        where = pl.ds(i * part, part)
        parts.append(pltpu.make_async_copy(rows_in.at[where], rows.at[where], rows_done.at[i]))
        parts[-1].start()
    tags[total:, :] = jnp.zeros_like(tags[total:, :])
    wide[total:, :] = jnp.zeros_like(wide[total:, :])
    small[0].wait()
    small[1].wait()
    local = jnp.bitwise_and(owner[...], CL_GRP - 1).astype(f32) + 1.0
    local = to_column(local, LANES)
    square = (LANES, LANES)
    for q in range(labels.shape[0]):
        hit = jnp.where(iota(square, 0) == labels[q : q + 1, :], local, 0.0)
        column = to_column(jnp.sum(hit, axis=0, keepdims=True), LANES)
        tags[q * LANES : (q + 1) * LANES, :] = jnp.broadcast_to(column, square)
    for i in range(ROW_PARTS):
        parts[i].wait()
        wide[i * part : (i + 1) * part, :] = rows[i * part : (i + 1) * part, :].astype(f32)
    small[2].wait()
    small[3].wait()
    head_base = jnp.bitwise_and(me[0], 3) * HEAD
    tail_base = jnp.bitwise_and(me[0], 15) * (CAP - HEAD)

    def one(g, carry):
        first = offsets[0, g]
        count = counts[0, g]
        window = pl.ds(pl.multiple_of(first - jnp.bitwise_and(first, 7), 8), WINDOW)
        back = WINDOW - jnp.bitwise_and(first, 7)
        picked = pltpu.roll(wide[window, :], back, 0)[:CAP]
        picked = jnp.where(iota((CAP, 1), 0) < count, picked, 0.0)
        for i in range(CHUNKS):
            out[g, i * HEAD : (i + 1) * HEAD, :] = picked[:HEAD, chunk(i)].astype(bf16)
        for q in range(CHUNKS // 2):
            both = jnp.concatenate([picked[HEAD:, chunk(2 * q)], picked[HEAD:, chunk(2 * q + 1)]], axis=0)
            start = CHUNKS * HEAD + 16 * q
            out[g, start : start + 16, :] = both.astype(bf16)
        tag = pltpu.roll(tags[window, :], back, 0)[:CAP]
        sub, lane = iota((CAP, LANES), 0), iota((CAP, LANES), 1)
        place = jnp.where(sub < HEAD, sub + head_base, sub - HEAD + tail_base)
        tag = jnp.where((lane == place) & (sub < count), tag, 0.0)
        head = jnp.sum(tag[:HEAD], axis=0, keepdims=True)
        tail = jnp.sum(tag[HEAD:], axis=0, keepdims=True)
        which = iota((TAG_ROWS, LANES), 0)
        tile = jnp.where(which == 0, head, jnp.where(which == 1, tail, 0.0))
        out[g, SEND_ROWS - TAG_ROWS :, :] = tile.astype(bf16)
        return carry

    batch = GROUPS // OUT_PARTS
    sent = []
    for i in range(OUT_PARTS):
        lax.fori_loop(i * batch, (i + 1) * batch, one, 0, unroll=4)
        where = pl.ds(i * batch, batch)
        sent.append(pltpu.make_async_copy(out.at[where], out_far.at[where], out_done.at[i]))
        sent[-1].start()
    for copy in sent:
        copy.wait()


def front(me, counts, offsets, labels, owner, rows):
    spare = rows.shape[0] + WINDOW
    labels = labels.reshape(-1, LANES)
    owner = owner.reshape(1, -1)
    sent = (GROUPS, SEND_ROWS, LANES)
    return pl.pallas_call(
        front_kernel,
        out_shape=jax.ShapeDtypeStruct(sent, bf16),
        in_specs=[SCALARS] + [FAR] * 5,
        out_specs=FAR,
        scratch_shapes=[
            pltpu.SMEM(counts.shape, jnp.int32),
            pltpu.SMEM(offsets.shape, jnp.int32),
            pltpu.VMEM(labels.shape, jnp.int32),
            pltpu.VMEM(owner.shape, jnp.int32),
            pltpu.VMEM(rows.shape, bf16),
            pltpu.VMEM((spare, rows.shape[1]), f32),
            pltpu.VMEM((spare, LANES), f32),
            pltpu.VMEM(sent, bf16),
            pltpu.SemaphoreType.DMA((4,)),
            pltpu.SemaphoreType.DMA((ROW_PARTS,)),
            pltpu.SemaphoreType.DMA((OUT_PARTS,)),
        ],
        name="front",
    )(me, counts, offsets, labels, owner, rows)


def pack_rows(pieces, lasts):
    parts = [jnp.concatenate([pieces[2 * q], pieces[2 * q + 1]], axis=0) for q in range(CHUNKS // 2)]
    which = iota((8, LANES), 0)
    end = jnp.zeros((8, LANES), f32)
    for i in range(CHUNKS):
        end = jnp.where(which == i, lasts[i], end)
    return parts, end


def pack_kernel(rows, out):
    wide = rows[...].astype(f32)
    pieces = [wide[:24, chunk(i)] for i in range(CHUNKS)]
    lasts = [wide[24:25, chunk(i)] for i in range(CHUNKS)]
    parts, end = pack_rows(pieces, lasts)
    for q in range(CHUNKS // 2):
        out[0, 48 * q : 48 * q + 48, :] = parts[q].astype(bf16)
    out[0, 144:, :] = end.astype(bf16)


def pack(rows):
    return pl.pallas_call(
        pack_kernel,
        out_shape=jax.ShapeDtypeStruct((1, PACK, LANES), bf16),
        in_specs=[ON_CHIP],
        out_specs=ON_CHIP,
        compiler_params=pltpu.CompilerParams(vmem_limit_bytes=4 * 2**20),
        name="pack",
    )(rows)


def unpack_items(arrived, items, tags):
    def head(s, carry):
        for i in range(CHUNKS):
            items[pl.ds(pl.multiple_of(s * HEAD, HEAD), HEAD), chunk(i)] = arrived[s, i * HEAD : (i + 1) * HEAD, :]
        return carry

    lax.fori_loop(0, GROUPS, head, 0, unroll=4)

    def tail(u, carry):
        rows = pl.ds(pl.multiple_of(GROUPS * HEAD + 16 * u, 16), 16)
        for q in range(CHUNKS // 2):
            start = CHUNKS * HEAD + 16 * q
            even = arrived[2 * u, start : start + 16, :].astype(f32)
            odd = arrived[2 * u + 1, start : start + 16, :].astype(f32)
            items[rows, chunk(2 * q)] = jnp.concatenate([even[:8], odd[:8]], axis=0).astype(bf16)
            items[rows, chunk(2 * q + 1)] = jnp.concatenate([even[8:], odd[8:]], axis=0).astype(bf16)
        return carry

    lax.fori_loop(0, GROUPS // 2, tail, 0, unroll=4)

    def tag_tile(s):
        return arrived[s, SEND_ROWS - TAG_ROWS :, :].astype(f32)

    pieces = []
    for u in range(GROUPS // 4):
        tile = sum(tag_tile(4 * u + i) for i in range(4))
        pieces.append(tile[0:1])
    for v in range(GROUPS // 16):
        tile = sum(tag_tile(16 * v + i) for i in range(16))
        pieces.append(tile[1:2])
    tags[...] = jnp.concatenate(pieces, axis=1) - 1.0


def pack_sums(out, sums, lasts, totals, half):
    which = iota((8, LANES), 0)
    for z in range(ZS):
        end = jnp.zeros((8, LANES), f32)
        last = last_row(half, z)
        for i in range(CHUNKS):
            out[z, 24 * i : 24 * i + 24, :] = sums[24 * z : 24 * z + 24, chunk(i)]
            end = jnp.where(which == i, lasts[last : last + 1, chunk(i)], end)
        out[z, 144:, :] = jnp.where(which == 6, totals[z], end)


def last_row(half, z):
    return 8 * (z // 2) + 2 * half + z % 2


def sweep_kernel(first, core, *refs):
    if first:
        arrived, blocks, send, weights, marks, items, tags, panel, sums = refs
        unpack_items(arrived, items, tags)
    else:
        items, tags, blocks, send, weights, marks, panel, sums = refs

    lengths = []
    ends = []
    for half in range(2):
        for pair in range(ZS // 2):
            squares = [jnp.zeros((24, LANES), f32) for _ in range(2)]
            parts = []
            for n in range(2):
                source = 2 * (2 * pair + n) + jnp.bitwise_xor(core[0], half)
                ends.append(blocks[source, 144:, :].astype(f32))
                pieces = []
                for q in range(CHUNKS // 2):
                    part = blocks[source, 48 * q : 48 * q + 48, :].astype(f32)
                    pieces += [part[:24], part[24:]]
                for piece in pieces:
                    squares[n] = squares[n] + piece * piece
                parts.append(pieces)
            start = half * MAIN + 48 * pair
            for i in range(CHUNKS):
                both = jnp.concatenate([parts[0][i], parts[1][i]], axis=0)
                panel[start : start + 48, chunk(i)] = both.astype(bf16)
            lengths += [jnp.sum(square, axis=1, keepdims=True) for square in squares]
    square = jnp.zeros((LASTS, LANES), f32)
    which = iota((LASTS, LANES), 0)
    for i in range(CHUNKS):
        piece = jnp.zeros((LASTS, LANES), f32)
        for half in range(2):
            for z in range(ZS):
                row = ends[half * ZS + z][i : i + 1]
                piece = jnp.where(which == last_row(half, z), row, piece)
        square = square + piece * piece
        panel[2 * MAIN :, chunk(i)] = piece.astype(bf16)
    lengths.append(jnp.sum(square, axis=1, keepdims=True))
    lengths = jnp.concatenate(lengths, axis=0) * (1.0 / temper)

    starts = [(0, 48), (MAIN, 48), (2 * MAIN, 8)]
    real = iota((8, 1), 0) < 4
    totals = [[jnp.zeros((rows, LANES), f32) for _ in range(CL_GRP)] for _, rows in starts]
    for j in range(ITEMS // STEP):
        columns = slice(j * STEP, (j + 1) * STEP)
        product = lax.dot_general(
            panel[...], items[columns, :], (((1,), (1,)), ((), ())), preferred_element_type=f32
        )
        logits = product * (2.0 / temper) - lengths
        tag = tags[:, columns]
        picked = []
        for start, rows in starts:
            chosen = logits[start : start + rows]
            for c in range(1, CL_GRP):
                chosen = jnp.where(tag == c, logits[start + c * rows : start + (c + 1) * rows], chosen)
            picked.append(chosen)
        picked[2] = jnp.where(real, picked[2], -3e38)
        highest = functools.reduce(jnp.maximum, [jnp.max(p, axis=0, keepdims=True) for p in picked])
        exponent = [jnp.exp(p - highest) for p in picked]
        scale = 1.0 / sum(jnp.sum(e, axis=0, keepdims=True) for e in exponent)
        for n, (start, rows) in enumerate(starts):
            weight = exponent[n] * scale
            owned = [jnp.where(tag == c, weight, 0.0) for c in range(CL_GRP)]
            for c in range(CL_GRP):
                for i in range(STEP // LANES):
                    totals[n][c] = totals[n][c] + owned[c][:, chunk(i)]
            if rows % 16:
                owned = [jnp.concatenate(owned[c : c + 2], axis=0) for c in range(0, CL_GRP, 2)]
            for c, part in enumerate(owned):
                size = part.shape[0]
                weights[start + c * size : start + (c + 1) * size, columns] = part.astype(bf16)

    lane = iota((1, LANES), 1)
    rows_of = [[], []]
    for half in range(2):
        for z in range(ZS):
            c, n = z // 2, z % 2
            main = to_row(jnp.sum(totals[half][c][24 * n : 24 * n + 24], axis=1, keepdims=True))
            last = jnp.sum(totals[2][c], axis=1, keepdims=True)[2 * half + n : 2 * half + n + 1]
            rows_of[half].append(jnp.where(lane == 24, last, main))
    for z in range(ZS):
        marks[z, :, :] = jnp.broadcast_to(rows_of[0][z], (8, LANES))
    sums[...] = jnp.dot(weights[MAIN:, :], items[...], preferred_element_type=f32)
    pack_sums(send, sums, sums.at[MAIN:], rows_of[1], 1)


def sweep(core, passages, blocks, first):
    out_shape = [
        jax.ShapeDtypeStruct((ZS, PACK, LANES), f32),
        jax.ShapeDtypeStruct((PANEL, ITEMS), bf16),
        jax.ShapeDtypeStruct((ZS, 8, LANES), f32),
    ]
    if first:
        out_shape.append(jax.ShapeDtypeStruct((ITEMS, CHUNKS * LANES), bf16))
        out_shape.append(jax.ShapeDtypeStruct((1, ITEMS), f32))
    return pl.pallas_call(
        functools.partial(sweep_kernel, first),
        out_shape=out_shape,
        in_specs=[SCALARS] + [ON_CHIP] * (len(passages) + 1),
        out_specs=[ON_CHIP] * len(out_shape),
        scratch_shapes=[
            pltpu.VMEM((PANEL, CHUNKS * LANES), bf16),
            pltpu.VMEM((MAIN + LASTS, CHUNKS * LANES), f32),
        ],
        compiler_params=pltpu.CompilerParams(vmem_limit_bytes=32 * 2**20),
        name="sweep",
    )(core, *passages, blocks)


def kept_kernel(weights, items, marks, keep, sums, lasts):
    sums[...] = jnp.dot(weights[:MAIN, :], items[...], preferred_element_type=f32)
    lasts[...] = jnp.dot(weights[2 * MAIN :, :], items[...], preferred_element_type=f32)
    pack_sums(keep, sums, lasts, [marks[z, :, :] for z in range(ZS)], 0)


def kept(weights, items, marks):
    features = CHUNKS * LANES
    return pl.pallas_call(
        kept_kernel,
        out_shape=jax.ShapeDtypeStruct((ZS, PACK, LANES), f32),
        in_specs=[ON_CHIP] * 3,
        out_specs=ON_CHIP,
        scratch_shapes=[pltpu.VMEM((MAIN, features), f32), pltpu.VMEM((LASTS, features), f32)],
        cost_estimate=pl.CostEstimate(
            flops=2 * (MAIN + LASTS) * ITEMS * features, bytes_accessed=4 * 2**20, transcendentals=0
        ),
        compiler_params=pltpu.CompilerParams(vmem_limit_bytes=16 * 2**20),
        name="kept",
    )(weights, items, marks)


def join_kernel(keep, received, out):
    which = iota((8, LANES), 0)
    for z in range(ZS):
        out[z, :144, :] = (keep[z, :144, :] + received[z, :144, :]).astype(bf16)
        end = keep[z, 144:152, :] + received[z, 144:152, :]
        rest = end - end.astype(bf16).astype(f32)
        end = jnp.where(which == 7, rest[6:7], end)
        out[z, 144:, :] = end.astype(bf16)


def join(keep, received):
    return pl.pallas_call(
        join_kernel,
        out_shape=jax.ShapeDtypeStruct((ZS, PACK, LANES), bf16),
        in_specs=[ON_CHIP] * 2,
        out_specs=ON_CHIP,
        compiler_params=pltpu.CompilerParams(vmem_limit_bytes=8 * 2**20),
        name="join",
    )(keep, received)


def update_kernel(parts, prior, out, *packed):
    total = parts[0].astype(f32)
    for z in range(1, ZS):
        total = total + parts[z].astype(f32)
    end = total[144:152]
    weight = to_column(end[6:7] + end[7:8], BLOCK) + 1.0
    before = prior[...].astype(f32)
    pieces, lasts = [], []
    for i in range(CHUNKS):
        piece = (total[24 * i : 24 * i + 24] + before[:24, chunk(i)]) / weight[:24]
        last = (end[i : i + 1] + before[24:25, chunk(i)]) / weight[24:25]
        out[:24, chunk(i)] = piece
        out[24:25, chunk(i)] = last
        pieces.append(piece)
        lasts.append(last)
    if packed:
        parts, end = pack_rows(pieces, lasts)
        for q in range(CHUNKS // 2):
            packed[0][0, 48 * q : 48 * q + 48, :] = parts[q].astype(bf16)
        packed[0][0, 144:, :] = end.astype(bf16)


def update(parts, prior, last):
    out_shape = [jax.ShapeDtypeStruct((OWN, CHUNKS * LANES), f32)]
    if not last:
        out_shape.append(jax.ShapeDtypeStruct((1, PACK, LANES), bf16))
    return pl.pallas_call(
        update_kernel,
        out_shape=out_shape,
        in_specs=[ON_CHIP] * 2,
        out_specs=[ON_CHIP] * len(out_shape),
        compiler_params=pltpu.CompilerParams(vmem_limit_bytes=8 * 2**20),
        name="update",
    )(parts, prior)


def shards(passages, labels, send_counts, send_offsets, owner_slot, centroids):
    members = lax.axis_size("member")
    along_z = [[m for m in range(members) if m % 2 == core] for core in range(2)]
    cores = [(m, m ^ 1) for m in range(members)]
    me = lax.axis_index("group").reshape(1).astype(jnp.int32)
    core = jnp.bitwise_and(lax.axis_index("member"), 1).reshape(1).astype(jnp.int32)

    outgoing = front(me, send_counts, send_offsets, labels, owner_slot, passages)
    passage_refs = [lax.all_to_all(outgoing, "group", split_axis=0, concat_axis=0, tiled=True)]
    packed = pack(centroids)
    prior = centroids
    for turn in range(ITERS):
        blocks = lax.all_gather(packed, "member", axis=0, tiled=True)
        send, weights, marks, *unpacked = sweep(core, passage_refs, blocks, turn == 0)
        passage_refs = unpacked or passage_refs
        received = lax.ppermute(send, "member", cores)
        keep = kept(weights, passage_refs[0], marks)
        parts = lax.all_to_all(
            join(keep, received), "member", split_axis=0, concat_axis=0, tiled=True, axis_index_groups=along_z
        )
        prior, *packed = update(parts, prior, turn == ITERS - 1)
        packed = packed[0] if packed else None
    return prior


def solution(mesh):
    spec = P(("group", "member"))
    rows = P(("group", "member"), None)
    return jax.shard_map(
        shards,
        mesh=mesh,
        in_specs=(rows, spec, rows, rows, P(), rows),
        out_specs=rows,
        check_vma=False,
    )
```

```python
import functools

import jax
import jax.numpy as jnp
from jax import lax
from jax.experimental import pallas as pl
from jax.experimental.pallas import tpu as pltpu
from jax.sharding import PartitionSpec as P

K = 100
CL_GRP = 4
ITERS = 2
temper = 16.0

GROUPS = 32
CAP = 40
WINDOW = CAP + 8
HEAD = 32
LANES = 128
CHUNKS = 6
TAG_ROWS = 8
SEND_ROWS = 240 + TAG_ROWS
ROW_PARTS = 4
OUT_PARTS = 8
ZS = 8
OWN = 25
BLOCK = 32
PACK = 152
MAIN = ZS * 24
LASTS = 32
PANEL = 2 * MAIN + LASTS
ITEMS = GROUPS * CAP
HELD = ITEMS + 16
STEP = 256
f32 = jnp.float32
bf16 = jnp.bfloat16

ON_CHIP = pl.BlockSpec(memory_space=pltpu.VMEM)
FAR = pl.BlockSpec(memory_space=pltpu.HBM)
SCALARS = pl.BlockSpec(memory_space=pltpu.SMEM)


def iota(shape, axis):
    return lax.broadcasted_iota(jnp.int32, shape, axis)


def chunk(i):
    return slice(i * LANES, (i + 1) * LANES)


def to_column(row, rows):
    shape = (rows, LANES)
    return jnp.sum(jnp.where(iota(shape, 0) == iota(shape, 1), row, 0.0), axis=1, keepdims=True)


def to_row(column):
    shape = (column.shape[0], LANES)
    return jnp.sum(jnp.where(iota(shape, 0) == iota(shape, 1), column, 0.0), axis=0, keepdims=True)


def front_kernel(me, counts_in, offsets_in, labels_in, owner_in, rows_in, out_far, *scratch):
    counts, offsets, labels, owner, rows, wide, tags, out, small_done, rows_done, out_done = scratch
    total = rows.shape[0]
    part = total // ROW_PARTS
    small = [
        pltpu.make_async_copy(source, target, small_done.at[i])
        for i, (source, target) in enumerate(
            ((labels_in, labels), (owner_in, owner), (counts_in, counts), (offsets_in, offsets))
        )
    ]
    for copy in small:
        copy.start()
    parts = []
    for i in range(ROW_PARTS):
        where = pl.ds(i * part, part)
        parts.append(pltpu.make_async_copy(rows_in.at[where], rows.at[where], rows_done.at[i]))
        parts[-1].start()
    tags[total:, :] = jnp.zeros_like(tags[total:, :])
    wide[total:, :] = jnp.zeros_like(wide[total:, :])
    small[0].wait()
    small[1].wait()
    local = jnp.bitwise_and(owner[...], CL_GRP - 1).astype(f32) + 1.0
    local = to_column(local, LANES)
    square = (LANES, LANES)
    for q in range(labels.shape[0]):
        hit = jnp.where(iota(square, 0) == labels[q : q + 1, :], local, 0.0)
        column = to_column(jnp.sum(hit, axis=0, keepdims=True), LANES)
        tags[q * LANES : (q + 1) * LANES, :] = jnp.broadcast_to(column, square)
    for i in range(ROW_PARTS):
        parts[i].wait()
        wide[i * part : (i + 1) * part, :] = rows[i * part : (i + 1) * part, :].astype(f32)
    small[2].wait()
    small[3].wait()
    head_base = jnp.bitwise_and(me[0], 3) * HEAD
    tail_base = jnp.bitwise_and(me[0], 15) * (CAP - HEAD)

    def one(g, carry):
        first = offsets[0, g]
        count = counts[0, g]
        window = pl.ds(pl.multiple_of(first - jnp.bitwise_and(first, 7), 8), WINDOW)
        back = WINDOW - jnp.bitwise_and(first, 7)
        picked = pltpu.roll(wide[window, :], back, 0)[:CAP]
        picked = jnp.where(iota((CAP, 1), 0) < count, picked, 0.0)
        for i in range(CHUNKS):
            out[g, i * HEAD : (i + 1) * HEAD, :] = picked[:HEAD, chunk(i)].astype(bf16)
        for q in range(CHUNKS // 2):
            both = jnp.concatenate([picked[HEAD:, chunk(2 * q)], picked[HEAD:, chunk(2 * q + 1)]], axis=0)
            start = CHUNKS * HEAD + 16 * q
            out[g, start : start + 16, :] = both.astype(bf16)
        tag = pltpu.roll(tags[window, :], back, 0)[:CAP]
        sub, lane = iota((CAP, LANES), 0), iota((CAP, LANES), 1)
        place = jnp.where(sub < HEAD, sub + head_base, sub - HEAD + tail_base)
        tag = jnp.where((lane == place) & (sub < count), tag, 0.0)
        head = jnp.sum(tag[:HEAD], axis=0, keepdims=True)
        tail = jnp.sum(tag[HEAD:], axis=0, keepdims=True)
        which = iota((TAG_ROWS, LANES), 0)
        tile = jnp.where(which == 0, head, jnp.where(which == 1, tail, 0.0))
        out[g, SEND_ROWS - TAG_ROWS :, :] = tile.astype(bf16)
        return carry

    batch = GROUPS // OUT_PARTS
    sent = []
    for i in range(OUT_PARTS):
        lax.fori_loop(i * batch, (i + 1) * batch, one, 0, unroll=4)
        where = pl.ds(i * batch, batch)
        sent.append(pltpu.make_async_copy(out.at[where], out_far.at[where], out_done.at[i]))
        sent[-1].start()
    for copy in sent:
        copy.wait()


def front(me, counts, offsets, labels, owner, rows):
    spare = rows.shape[0] + WINDOW
    labels = labels.reshape(-1, LANES)
    owner = owner.reshape(1, -1)
    sent = (GROUPS, SEND_ROWS, LANES)
    return pl.pallas_call(
        front_kernel,
        out_shape=jax.ShapeDtypeStruct(sent, bf16),
        in_specs=[SCALARS] + [FAR] * 5,
        out_specs=FAR,
        scratch_shapes=[
            pltpu.SMEM(counts.shape, jnp.int32),
            pltpu.SMEM(offsets.shape, jnp.int32),
            pltpu.VMEM(labels.shape, jnp.int32),
            pltpu.VMEM(owner.shape, jnp.int32),
            pltpu.VMEM(rows.shape, bf16),
            pltpu.VMEM((spare, rows.shape[1]), f32),
            pltpu.VMEM((spare, LANES), f32),
            pltpu.VMEM(sent, bf16),
            pltpu.SemaphoreType.DMA((4,)),
            pltpu.SemaphoreType.DMA((ROW_PARTS,)),
            pltpu.SemaphoreType.DMA((OUT_PARTS,)),
        ],
        name="front",
    )(me, counts, offsets, labels, owner, rows)


def pack_rows(pieces, lasts):
    parts = [jnp.concatenate([pieces[2 * q], pieces[2 * q + 1]], axis=0) for q in range(CHUNKS // 2)]
    which = iota((8, LANES), 0)
    end = jnp.zeros((8, LANES), f32)
    for i in range(CHUNKS):
        end = jnp.where(which == i, lasts[i], end)
    return parts, end


def pack_kernel(rows, out):
    wide = rows[...].astype(f32)
    pieces = [wide[:24, chunk(i)] for i in range(CHUNKS)]
    lasts = [wide[24:25, chunk(i)] for i in range(CHUNKS)]
    parts, end = pack_rows(pieces, lasts)
    for q in range(CHUNKS // 2):
        out[0, 48 * q : 48 * q + 48, :] = parts[q].astype(bf16)
    out[0, 144:, :] = end.astype(bf16)


def pack(rows):
    return pl.pallas_call(
        pack_kernel,
        out_shape=jax.ShapeDtypeStruct((1, PACK, LANES), bf16),
        in_specs=[ON_CHIP],
        out_specs=ON_CHIP,
        compiler_params=pltpu.CompilerParams(vmem_limit_bytes=4 * 2**20),
        name="pack",
    )(rows)


def unpack_items(arrived, items, tags):
    def head(s, carry):
        for i in range(CHUNKS):
            items[pl.ds(pl.multiple_of(s * HEAD, HEAD), HEAD), chunk(i)] = arrived[s, i * HEAD : (i + 1) * HEAD, :]
        return carry

    lax.fori_loop(0, GROUPS, head, 0, unroll=4)

    def tail(u, carry):
        rows = pl.ds(pl.multiple_of(GROUPS * HEAD + 16 * u, 16), 16)
        for q in range(CHUNKS // 2):
            start = CHUNKS * HEAD + 16 * q
            even = arrived[2 * u, start : start + 16, :].astype(f32)
            odd = arrived[2 * u + 1, start : start + 16, :].astype(f32)
            items[rows, chunk(2 * q)] = jnp.concatenate([even[:8], odd[:8]], axis=0).astype(bf16)
            items[rows, chunk(2 * q + 1)] = jnp.concatenate([even[8:], odd[8:]], axis=0).astype(bf16)
        return carry

    lax.fori_loop(0, GROUPS // 2, tail, 0, unroll=4)

    def tag_tile(s):
        return arrived[s, SEND_ROWS - TAG_ROWS :, :].astype(f32)

    pieces = []
    for u in range(GROUPS // 4):
        tile = sum(tag_tile(4 * u + i) for i in range(4))
        pieces.append(tile[0:1])
    for v in range(GROUPS // 16):
        tile = sum(tag_tile(16 * v + i) for i in range(16))
        pieces.append(tile[1:2])
    tags[...] = jnp.concatenate(pieces, axis=1) - 1.0
    rows = [
        jnp.concatenate([tags[:, start : start + ITEMS // 2], jnp.zeros((1, LANES), f32)], axis=1)
        for start in (0, ITEMS // 2)
    ]
    which = iota((HELD - ITEMS, CHUNKS * LANES), 0)
    held = jnp.where(which == 0, rows[0], jnp.where(which == 1, rows[1], 0.0))
    items[ITEMS:, :] = held.astype(bf16)


def pack_sums(out, sums, lasts, totals, half):
    which = iota((8, LANES), 0)
    for z in range(ZS):
        end = jnp.zeros((8, LANES), f32)
        last = last_row(half, z)
        for i in range(CHUNKS):
            out[z, 24 * i : 24 * i + 24, :] = sums[24 * z : 24 * z + 24, chunk(i)]
            end = jnp.where(which == i, lasts[last : last + 1, chunk(i)], end)
        out[z, 144:, :] = jnp.where(which == 6, totals[z], end)


def last_row(half, z):
    return 8 * (z // 2) + 2 * half + z % 2


def sweep_kernel(core, arrived, blocks, send, weights, marks, items, tags, panel, sums):
    unpack_items(arrived, items, tags)
    lengths = []
    ends = []
    for half in range(2):
        for pair in range(ZS // 2):
            squares = [jnp.zeros((24, LANES), f32) for _ in range(2)]
            parts = []
            for n in range(2):
                source = 2 * (2 * pair + n) + jnp.bitwise_xor(core[0], half)
                ends.append(blocks[source, 144:, :].astype(f32))
                pieces = []
                for q in range(CHUNKS // 2):
                    part = blocks[source, 48 * q : 48 * q + 48, :].astype(f32)
                    pieces += [part[:24], part[24:]]
                for piece in pieces:
                    squares[n] = squares[n] + piece * piece
                parts.append(pieces)
            start = half * MAIN + 48 * pair
            for i in range(CHUNKS):
                both = jnp.concatenate([parts[0][i], parts[1][i]], axis=0)
                panel[start : start + 48, chunk(i)] = both.astype(bf16)
            lengths += [jnp.sum(square, axis=1, keepdims=True) for square in squares]
    square = jnp.zeros((LASTS, LANES), f32)
    which = iota((LASTS, LANES), 0)
    for i in range(CHUNKS):
        piece = jnp.zeros((LASTS, LANES), f32)
        for half in range(2):
            for z in range(ZS):
                row = ends[half * ZS + z][i : i + 1]
                piece = jnp.where(which == last_row(half, z), row, piece)
        square = square + piece * piece
        panel[2 * MAIN :, chunk(i)] = piece.astype(bf16)
    lengths.append(jnp.sum(square, axis=1, keepdims=True))
    lengths = jnp.concatenate(lengths, axis=0) * (1.0 / temper)

    starts = [(0, 48), (MAIN, 48), (2 * MAIN, 8)]
    real = iota((8, 1), 0) < 4
    totals = [[jnp.zeros((rows, LANES), f32) for _ in range(CL_GRP)] for _, rows in starts]
    for j in range(ITEMS // STEP):
        columns = slice(j * STEP, (j + 1) * STEP)
        product = lax.dot_general(
            panel[...], items[columns, :], (((1,), (1,)), ((), ())), preferred_element_type=f32
        )
        logits = product * (2.0 / temper) - lengths
        tag = tags[:, columns]
        picked = []
        for start, rows in starts:
            chosen = logits[start : start + rows]
            for c in range(1, CL_GRP):
                chosen = jnp.where(tag == c, logits[start + c * rows : start + (c + 1) * rows], chosen)
            picked.append(chosen)
        picked[2] = jnp.where(real, picked[2], -3e38)
        highest = functools.reduce(jnp.maximum, [jnp.max(p, axis=0, keepdims=True) for p in picked])
        exponent = [jnp.exp(p - highest) for p in picked]
        scale = 1.0 / sum(jnp.sum(e, axis=0, keepdims=True) for e in exponent)
        for n, (start, rows) in enumerate(starts):
            weight = exponent[n] * scale
            owned = [jnp.where(tag == c, weight, 0.0) for c in range(CL_GRP)]
            for c in range(CL_GRP):
                for i in range(STEP // LANES):
                    totals[n][c] = totals[n][c] + owned[c][:, chunk(i)]
            if rows % 16:
                owned = [jnp.concatenate(owned[c : c + 2], axis=0) for c in range(0, CL_GRP, 2)]
            for c, part in enumerate(owned):
                size = part.shape[0]
                weights[start + c * size : start + (c + 1) * size, columns] = part.astype(bf16)

    lane = iota((1, LANES), 1)
    rows_of = [[], []]
    for half in range(2):
        for z in range(ZS):
            c, n = z // 2, z % 2
            main = to_row(jnp.sum(totals[half][c][24 * n : 24 * n + 24], axis=1, keepdims=True))
            last = jnp.sum(totals[2][c], axis=1, keepdims=True)[2 * half + n : 2 * half + n + 1]
            rows_of[half].append(jnp.where(lane == 24, last, main))
    for z in range(ZS):
        marks[z, :, :] = jnp.broadcast_to(rows_of[0][z], (8, LANES))
    sums[...] = jnp.dot(weights[MAIN:, :], items[:ITEMS, :], preferred_element_type=f32)
    pack_sums(send, sums, sums.at[MAIN:], rows_of[1], 1)


def sweep(core, arrived, blocks):
    out_shape = [
        jax.ShapeDtypeStruct((ZS, PACK, LANES), f32),
        jax.ShapeDtypeStruct((PANEL, ITEMS), bf16),
        jax.ShapeDtypeStruct((ZS, 8, LANES), f32),
        jax.ShapeDtypeStruct((HELD, CHUNKS * LANES), bf16),
    ]
    return pl.pallas_call(
        sweep_kernel,
        out_shape=out_shape,
        in_specs=[SCALARS, ON_CHIP, ON_CHIP],
        out_specs=[ON_CHIP] * len(out_shape),
        scratch_shapes=[
            pltpu.VMEM((1, ITEMS), f32),
            pltpu.VMEM((PANEL, CHUNKS * LANES), bf16),
            pltpu.VMEM((MAIN + LASTS, CHUNKS * LANES), f32),
        ],
        compiler_params=pltpu.CompilerParams(vmem_limit_bytes=32 * 2**20),
        name="sweep",
    )(core, arrived, blocks)


def kept_kernel(weights, items, marks, keep, sums, lasts):
    sums[...] = jnp.dot(weights[:MAIN, :], items[:ITEMS, :], preferred_element_type=f32)
    lasts[...] = jnp.dot(weights[2 * MAIN :, :], items[:ITEMS, :], preferred_element_type=f32)
    pack_sums(keep, sums, lasts, [marks[z, :, :] for z in range(ZS)], 0)


def kept(weights, items, marks):
    features = CHUNKS * LANES
    return pl.pallas_call(
        kept_kernel,
        out_shape=jax.ShapeDtypeStruct((ZS, PACK, LANES), f32),
        in_specs=[ON_CHIP] * 3,
        out_specs=ON_CHIP,
        scratch_shapes=[pltpu.VMEM((MAIN, features), f32), pltpu.VMEM((LASTS, features), f32)],
        cost_estimate=pl.CostEstimate(
            flops=2 * (MAIN + LASTS) * ITEMS * features, bytes_accessed=4 * 2**20, transcendentals=0
        ),
        compiler_params=pltpu.CompilerParams(vmem_limit_bytes=16 * 2**20),
        name="kept",
    )(weights, items, marks)


def held_tags(items):
    rows = items[ITEMS:, :].astype(f32)
    return jnp.concatenate([rows[n : n + 1, : ITEMS // 2] for n in range(2)], axis=1)


def half_kernel(items, others, mine, exponents, stats, panel):
    lengths = []
    ends = []
    for pair in range(ZS // 2):
        squares = [jnp.zeros((24, LANES), f32) for _ in range(2)]
        parts = []
        for n in range(2):
            z = 2 * pair + n
            ends.append(mine[z, 144:, :].astype(f32))
            pieces = []
            for q in range(CHUNKS // 2):
                part = mine[z, 48 * q : 48 * q + 48, :].astype(f32)
                pieces += [part[:24], part[24:]]
            for piece in pieces:
                squares[n] = squares[n] + piece * piece
            parts.append(pieces)
        for i in range(CHUNKS):
            both = jnp.concatenate([parts[0][i], parts[1][i]], axis=0)
            panel[48 * pair : 48 * pair + 48, chunk(i)] = both.astype(bf16)
        lengths += [jnp.sum(square, axis=1, keepdims=True) for square in squares]
    square = jnp.zeros((LASTS, LANES), f32)
    which = iota((LASTS, LANES), 0)
    for i in range(CHUNKS):
        piece = jnp.zeros((LASTS, LANES), f32)
        for z in range(ZS):
            piece = jnp.where(which == last_row(0, z), ends[z][i : i + 1], piece)
        square = square + piece * piece
        panel[MAIN:, chunk(i)] = piece.astype(bf16)
    lengths.append(jnp.sum(square, axis=1, keepdims=True))
    lengths = jnp.concatenate(lengths, axis=0) * (1.0 / temper)

    real = iota((8, 1), 0) < 2
    for side, source in enumerate((items, others)):
        tags = held_tags(source)
        for j in range(ITEMS // STEP):
            columns = slice(j * STEP, (j + 1) * STEP)
            product = lax.dot_general(
                panel[...], source[columns, :], (((1,), (1,)), ((), ())), preferred_element_type=f32
            )
            logits = product * (2.0 / temper) - lengths
            tag = tags[:, columns]
            picked = []
            for start, rows in ((0, 48), (MAIN, 8)):
                chosen = logits[start : start + rows]
                for c in range(1, CL_GRP):
                    chosen = jnp.where(tag == c, logits[start + c * rows : start + (c + 1) * rows], chosen)
                picked.append(chosen)
            picked[1] = jnp.where(real, picked[1], -3e38)
            highest = jnp.maximum(
                jnp.max(picked[0], axis=0, keepdims=True), jnp.max(picked[1], axis=0, keepdims=True)
            )
            main, last = [jnp.exp(p - highest) for p in picked]
            place = slice(side * ITEMS + j * STEP, side * ITEMS + (j + 1) * STEP)
            exponents[:48, place] = main
            exponents[48:, place] = last
            total = jnp.sum(main, axis=0, keepdims=True) + jnp.sum(last, axis=0, keepdims=True)
            stats[:, place] = jnp.where(iota((8, STEP), 0) == 0, highest, total)


def half_logits(items, others, mine):
    return pl.pallas_call(
        half_kernel,
        out_shape=[jax.ShapeDtypeStruct((56, 2 * ITEMS), f32), jax.ShapeDtypeStruct((8, 2 * ITEMS), f32)],
        in_specs=[ON_CHIP] * 3,
        out_specs=[ON_CHIP] * 2,
        scratch_shapes=[pltpu.VMEM((MAIN + LASTS, CHUNKS * LANES), bf16)],
        compiler_params=pltpu.CompilerParams(vmem_limit_bytes=32 * 2**20),
        name="half_logits",
    )(items, others, mine)


def half_sums_kernel(exponents, stats, theirs, items, others, out, weights, sums):
    totals = [jnp.zeros((48, LANES), f32) for _ in range(CL_GRP)]
    last_totals = [jnp.zeros((8, LANES), f32) for _ in range(CL_GRP)]
    for side, source in enumerate((items, others)):
        tags = held_tags(source)
        for j in range(ITEMS // STEP):
            tag = tags[:, j * STEP : (j + 1) * STEP]
            place = slice(side * ITEMS + j * STEP, side * ITEMS + (j + 1) * STEP)
            there = slice((1 - side) * ITEMS + j * STEP, (1 - side) * ITEMS + (j + 1) * STEP)
            top, other_top = stats[0:1, place], theirs[0:1, there]
            highest = jnp.maximum(top, other_top)
            share = jnp.exp(top - highest)
            whole = stats[1:2, place] * share + theirs[1:2, there] * jnp.exp(other_top - highest)
            scale = share / whole
            weight = exponents[:, place] * scale
            owned = [jnp.where(tag == c, weight, 0.0) for c in range(CL_GRP)]
            for c in range(CL_GRP):
                for i in range(STEP // LANES):
                    totals[c] = totals[c] + owned[c][:48, chunk(i)]
                    last_totals[c] = last_totals[c] + owned[c][48:, chunk(i)]
                weights[48 * c : 48 * c + 48, place] = owned[c][:48].astype(bf16)
            for c in range(0, CL_GRP, 2):
                both = jnp.concatenate([owned[c][48:], owned[c + 1][48:]], axis=0)
                weights[MAIN + 8 * c : MAIN + 8 * c + 16, place] = both.astype(bf16)
    sums[...] = jnp.dot(weights[:, :ITEMS], items[:ITEMS, :], preferred_element_type=f32) + jnp.dot(
        weights[:, ITEMS:], others[:ITEMS, :], preferred_element_type=f32
    )
    which = iota((8, LANES), 0)
    lane = iota((1, LANES), 1)
    for z in range(ZS):
        c, n = z // 2, z % 2
        row = MAIN + last_row(0, z)
        end = jnp.zeros((8, LANES), f32)
        for i in range(CHUNKS):
            end = jnp.where(which == i, sums[row : row + 1, chunk(i)], end)
        main = to_row(jnp.sum(totals[c][24 * n : 24 * n + 24], axis=1, keepdims=True))
        last = jnp.sum(last_totals[c], axis=1, keepdims=True)[n : n + 1]
        end = jnp.where(which == 6, jnp.where(lane == 24, last, main), end)
        for q in range(CHUNKS // 2):
            both = [sums[24 * z : 24 * z + 24, chunk(i)] for i in (2 * q, 2 * q + 1)]
            out[z, 48 * q : 48 * q + 48, :] = jnp.concatenate(both, axis=0).astype(bf16)
        out[z, 144:, :] = with_rest(end).astype(bf16)


def half_sums(exponents, stats, theirs, items, others):
    return pl.pallas_call(
        half_sums_kernel,
        out_shape=jax.ShapeDtypeStruct((ZS, PACK, LANES), bf16),
        in_specs=[ON_CHIP] * 5,
        out_specs=ON_CHIP,
        scratch_shapes=[
            pltpu.VMEM((MAIN + LASTS, 2 * ITEMS), bf16),
            pltpu.VMEM((MAIN + LASTS, CHUNKS * LANES), f32),
        ],
        compiler_params=pltpu.CompilerParams(vmem_limit_bytes=32 * 2**20),
        name="half_sums",
    )(exponents, stats, theirs, items, others)


def with_rest(end):
    rest = end - end.astype(bf16).astype(f32)
    return jnp.where(iota((8, LANES), 0) == 7, rest[6:7], end)


def join_kernel(keep, received, out):
    for z in range(ZS):
        out[z, :144, :] = (keep[z, :144, :] + received[z, :144, :]).astype(bf16)
        out[z, 144:, :] = with_rest(keep[z, 144:, :] + received[z, 144:, :]).astype(bf16)


def join(keep, received):
    return pl.pallas_call(
        join_kernel,
        out_shape=jax.ShapeDtypeStruct((ZS, PACK, LANES), bf16),
        in_specs=[ON_CHIP] * 2,
        out_specs=ON_CHIP,
        compiler_params=pltpu.CompilerParams(vmem_limit_bytes=8 * 2**20),
        name="join",
    )(keep, received)


def update_kernel(parts, prior, out, *copies):
    total = parts[0].astype(f32)
    for z in range(1, ZS):
        total = total + parts[z].astype(f32)
    end = total[144:152]
    weight = to_column(end[6:7] + end[7:8], BLOCK) + 1.0
    before = prior[...].astype(f32)
    pieces, lasts = [], []
    for i in range(CHUNKS):
        piece = (total[24 * i : 24 * i + 24] + before[:24, chunk(i)]) / weight[:24]
        last = (end[i : i + 1] + before[24:25, chunk(i)]) / weight[24:25]
        out[:24, chunk(i)] = piece
        out[24:25, chunk(i)] = last
        pieces.append(piece)
        lasts.append(last)
    if copies:
        parts, end = pack_rows(pieces, lasts)
        parts = [part.astype(bf16) for part in parts]
        end = end.astype(bf16)
        for z in range(ZS):
            for q in range(CHUNKS // 2):
                copies[0][z, 48 * q : 48 * q + 48, :] = parts[q]
            copies[0][z, 144:, :] = end


def update(parts, prior, last):
    out_shape = [jax.ShapeDtypeStruct((OWN, CHUNKS * LANES), f32)]
    if not last:
        out_shape.append(jax.ShapeDtypeStruct((ZS, PACK, LANES), bf16))
    return pl.pallas_call(
        update_kernel,
        out_shape=out_shape,
        in_specs=[ON_CHIP] * 2,
        out_specs=[ON_CHIP] * len(out_shape),
        compiler_params=pltpu.CompilerParams(vmem_limit_bytes=8 * 2**20),
        name="update",
    )(parts, prior)


def shards(passages, labels, send_counts, send_offsets, owner_slot, centroids):
    members = lax.axis_size("member")
    along_z = [[m for m in range(members) if m % 2 == core] for core in range(2)]
    cores = [(m, m ^ 1) for m in range(members)]
    me = lax.axis_index("group").reshape(1).astype(jnp.int32)
    core = jnp.bitwise_and(lax.axis_index("member"), 1).reshape(1).astype(jnp.int32)

    def along(blocks):
        return lax.all_to_all(
            blocks, "member", split_axis=0, concat_axis=0, tiled=True, axis_index_groups=along_z
        )

    outgoing = front(me, send_counts, send_offsets, labels, owner_slot, passages)
    arrived = lax.all_to_all(outgoing, "group", split_axis=0, concat_axis=0, tiled=True)
    blocks = lax.all_gather(pack(centroids), "member", axis=0, tiled=True)
    send, weights, marks, items = sweep(core, arrived, blocks)
    received = lax.ppermute(send, "member", cores)
    joined = join(kept(weights, items, marks), received)
    items, joined = lax.optimization_barrier((items, joined))
    others = lax.ppermute(items, "member", cores)
    current, copies = update(along(joined), centroids, False)
    exponents, stats = half_logits(items, others, along(copies))
    theirs = lax.ppermute(stats, "member", cores)
    (current,) = update(along(half_sums(exponents, stats, theirs, items, others)), current, True)
    return current


def solution(mesh):
    spec = P(("group", "member"))
    rows = P(("group", "member"), None)
    return jax.shard_map(
        shards,
        mesh=mesh,
        in_specs=(rows, spec, rows, rows, P(), rows),
        out_specs=rows,
        check_vma=False,
    )
```

```python
import functools

import jax
import jax.numpy as jnp
from jax import lax
from jax.experimental import pallas as pl
from jax.experimental.pallas import tpu as pltpu
from jax.sharding import PartitionSpec as P

K = 100
CL_GRP = 4
ITERS = 2
temper = 16.0

GROUPS = 32
CAP = 40
WINDOW = CAP + 8
HEAD = 32
LANES = 128
CHUNKS = 6
TAG_ROWS = 8
SEND_ROWS = 240 + TAG_ROWS
ROW_PARTS = 4
OUT_PARTS = 8
ZS = 8
OWN = 25
BLOCK = 32
PACK = 152
MAIN = ZS * 24
LASTS = 32
PANEL = 2 * MAIN + LASTS
ITEMS = GROUPS * CAP
STEP = 256
f32 = jnp.float32
bf16 = jnp.bfloat16

ON_CHIP = pl.BlockSpec(memory_space=pltpu.VMEM)
FAR = pl.BlockSpec(memory_space=pltpu.HBM)
SCALARS = pl.BlockSpec(memory_space=pltpu.SMEM)


def iota(shape, axis):
    return lax.broadcasted_iota(jnp.int32, shape, axis)


def chunk(i):
    return slice(i * LANES, (i + 1) * LANES)


def to_column(row, rows):
    shape = (rows, LANES)
    return jnp.sum(jnp.where(iota(shape, 0) == iota(shape, 1), row, 0.0), axis=1, keepdims=True)


def to_row(column):
    shape = (column.shape[0], LANES)
    return jnp.sum(jnp.where(iota(shape, 0) == iota(shape, 1), column, 0.0), axis=0, keepdims=True)


def front_kernel(me, counts_in, offsets_in, labels_in, owner_in, rows_in, out_far, *scratch):
    counts, offsets, labels, owner, rows, wide, tags, out, small_done, rows_done, out_done = scratch
    total = rows.shape[0]
    part = total // ROW_PARTS
    small = [
        pltpu.make_async_copy(source, target, small_done.at[i])
        for i, (source, target) in enumerate(
            ((labels_in, labels), (owner_in, owner), (counts_in, counts), (offsets_in, offsets))
        )
    ]
    for copy in small:
        copy.start()
    parts = []
    for i in range(ROW_PARTS):
        where = pl.ds(i * part, part)
        parts.append(pltpu.make_async_copy(rows_in.at[where], rows.at[where], rows_done.at[i]))
        parts[-1].start()
    tags[total:, :] = jnp.zeros_like(tags[total:, :])
    wide[total:, :] = jnp.zeros_like(wide[total:, :])
    small[0].wait()
    small[1].wait()
    local = jnp.bitwise_and(owner[...], CL_GRP - 1).astype(f32) + 1.0
    local = to_column(local, LANES)
    square = (LANES, LANES)
    for q in range(labels.shape[0]):
        hit = jnp.where(iota(square, 0) == labels[q : q + 1, :], local, 0.0)
        column = to_column(jnp.sum(hit, axis=0, keepdims=True), LANES)
        tags[q * LANES : (q + 1) * LANES, :] = jnp.broadcast_to(column, square)
    for i in range(ROW_PARTS):
        parts[i].wait()
        wide[i * part : (i + 1) * part, :] = rows[i * part : (i + 1) * part, :].astype(f32)
    small[2].wait()
    small[3].wait()
    head_base = jnp.bitwise_and(me[0], 3) * HEAD
    tail_base = jnp.bitwise_and(me[0], 15) * (CAP - HEAD)

    def one(g, carry):
        first = offsets[0, g]
        count = counts[0, g]
        window = pl.ds(pl.multiple_of(first - jnp.bitwise_and(first, 7), 8), WINDOW)
        back = WINDOW - jnp.bitwise_and(first, 7)
        picked = pltpu.roll(wide[window, :], back, 0)[:CAP]
        picked = jnp.where(iota((CAP, 1), 0) < count, picked, 0.0)
        for i in range(CHUNKS):
            out[g, i * HEAD : (i + 1) * HEAD, :] = picked[:HEAD, chunk(i)].astype(bf16)
        for q in range(CHUNKS // 2):
            both = jnp.concatenate([picked[HEAD:, chunk(2 * q)], picked[HEAD:, chunk(2 * q + 1)]], axis=0)
            start = CHUNKS * HEAD + 16 * q
            out[g, start : start + 16, :] = both.astype(bf16)
        tag = pltpu.roll(tags[window, :], back, 0)[:CAP]
        sub, lane = iota((CAP, LANES), 0), iota((CAP, LANES), 1)
        place = jnp.where(sub < HEAD, sub + head_base, sub - HEAD + tail_base)
        tag = jnp.where((lane == place) & (sub < count), tag, 0.0)
        head = jnp.sum(tag[:HEAD], axis=0, keepdims=True)
        tail = jnp.sum(tag[HEAD:], axis=0, keepdims=True)
        which = iota((TAG_ROWS, LANES), 0)
        tile = jnp.where(which == 0, head, jnp.where(which == 1, tail, 0.0))
        out[g, SEND_ROWS - TAG_ROWS :, :] = tile.astype(bf16)
        return carry

    batch = GROUPS // OUT_PARTS
    sent = []
    for i in range(OUT_PARTS):
        lax.fori_loop(i * batch, (i + 1) * batch, one, 0, unroll=4)
        where = pl.ds(i * batch, batch)
        sent.append(pltpu.make_async_copy(out.at[where], out_far.at[where], out_done.at[i]))
        sent[-1].start()
    for copy in sent:
        copy.wait()


def front(me, counts, offsets, labels, owner, rows):
    spare = rows.shape[0] + WINDOW
    labels = labels.reshape(-1, LANES)
    owner = owner.reshape(1, -1)
    sent = (GROUPS, SEND_ROWS, LANES)
    return pl.pallas_call(
        front_kernel,
        out_shape=jax.ShapeDtypeStruct(sent, bf16),
        in_specs=[SCALARS] + [FAR] * 5,
        out_specs=FAR,
        scratch_shapes=[
            pltpu.SMEM(counts.shape, jnp.int32),
            pltpu.SMEM(offsets.shape, jnp.int32),
            pltpu.VMEM(labels.shape, jnp.int32),
            pltpu.VMEM(owner.shape, jnp.int32),
            pltpu.VMEM(rows.shape, bf16),
            pltpu.VMEM((spare, rows.shape[1]), f32),
            pltpu.VMEM((spare, LANES), f32),
            pltpu.VMEM(sent, bf16),
            pltpu.SemaphoreType.DMA((4,)),
            pltpu.SemaphoreType.DMA((ROW_PARTS,)),
            pltpu.SemaphoreType.DMA((OUT_PARTS,)),
        ],
        name="front",
    )(me, counts, offsets, labels, owner, rows)


def pack_rows(pieces, lasts):
    parts = [jnp.concatenate([pieces[2 * q], pieces[2 * q + 1]], axis=0) for q in range(CHUNKS // 2)]
    which = iota((8, LANES), 0)
    end = jnp.zeros((8, LANES), f32)
    for i in range(CHUNKS):
        end = jnp.where(which == i, lasts[i], end)
    return parts, end


def pack_kernel(rows, out):
    wide = rows[...].astype(f32)
    pieces = [wide[:24, chunk(i)] for i in range(CHUNKS)]
    lasts = [wide[24:25, chunk(i)] for i in range(CHUNKS)]
    parts, end = pack_rows(pieces, lasts)
    for q in range(CHUNKS // 2):
        out[0, 48 * q : 48 * q + 48, :] = parts[q].astype(bf16)
    out[0, 144:, :] = end.astype(bf16)


def pack(rows):
    return pl.pallas_call(
        pack_kernel,
        out_shape=jax.ShapeDtypeStruct((1, PACK, LANES), bf16),
        in_specs=[ON_CHIP],
        out_specs=ON_CHIP,
        compiler_params=pltpu.CompilerParams(vmem_limit_bytes=4 * 2**20),
        name="pack",
    )(rows)


def unpack_items(arrived, items, tags):
    def head(s, carry):
        for i in range(CHUNKS):
            items[pl.ds(pl.multiple_of(s * HEAD, HEAD), HEAD), chunk(i)] = arrived[s, i * HEAD : (i + 1) * HEAD, :]
        return carry

    lax.fori_loop(0, GROUPS, head, 0, unroll=4)

    def tail(u, carry):
        rows = pl.ds(pl.multiple_of(GROUPS * HEAD + 16 * u, 16), 16)
        for q in range(CHUNKS // 2):
            start = CHUNKS * HEAD + 16 * q
            even = arrived[2 * u, start : start + 16, :].astype(f32)
            odd = arrived[2 * u + 1, start : start + 16, :].astype(f32)
            items[rows, chunk(2 * q)] = jnp.concatenate([even[:8], odd[:8]], axis=0).astype(bf16)
            items[rows, chunk(2 * q + 1)] = jnp.concatenate([even[8:], odd[8:]], axis=0).astype(bf16)
        return carry

    lax.fori_loop(0, GROUPS // 2, tail, 0, unroll=4)

    def tag_tile(s):
        return arrived[s, SEND_ROWS - TAG_ROWS :, :].astype(f32)

    pieces = []
    for u in range(GROUPS // 4):
        tile = sum(tag_tile(4 * u + i) for i in range(4))
        pieces.append(tile[0:1])
    for v in range(GROUPS // 16):
        tile = sum(tag_tile(16 * v + i) for i in range(16))
        pieces.append(tile[1:2])
    tags[...] = jnp.concatenate(pieces, axis=1) - 1.0


def pack_sums(out, sums, lasts, totals, half):
    which = iota((8, LANES), 0)
    for z in range(ZS):
        end = jnp.zeros((8, LANES), f32)
        last = last_row(half, z)
        for i in range(CHUNKS):
            out[z, 24 * i : 24 * i + 24, :] = sums[24 * z : 24 * z + 24, chunk(i)]
            end = jnp.where(which == i, lasts[last : last + 1, chunk(i)], end)
        out[z, 144:, :] = jnp.where(which == 6, totals[z], end)


def last_row(half, z):
    return 8 * (z // 2) + 2 * half + z % 2


def total_rows(main, last, half):
    rows = []
    for z in range(ZS):
        c, n = z // 2, z % 2
        row = to_row(jnp.sum(main[c][24 * n : 24 * n + 24], axis=1, keepdims=True))
        end = jnp.sum(last[c], axis=1, keepdims=True)[2 * half + n : 2 * half + n + 1]
        rows.append(jnp.where(iota((1, LANES), 1) == 24, end, row))
    return rows


def sweep_kernel(first, core, *refs):
    if first:
        arrived, blocks, send, weights, marks, items, tags, panel, sums = refs
        unpack_items(arrived, items, tags)
    else:
        items, tags, blocks, send, weights, marks, panel, sums = refs

    lengths = []
    ends = []
    for half in range(2):
        for pair in range(ZS // 2):
            squares = [jnp.zeros((24, LANES), f32) for _ in range(2)]
            parts = []
            for n in range(2):
                source = 2 * (2 * pair + n) + jnp.bitwise_xor(core[0], half)
                ends.append(blocks[source, 144:, :].astype(f32))
                pieces = []
                for q in range(CHUNKS // 2):
                    part = blocks[source, 48 * q : 48 * q + 48, :].astype(f32)
                    pieces += [part[:24], part[24:]]
                for piece in pieces:
                    squares[n] = squares[n] + piece * piece
                parts.append(pieces)
            start = half * MAIN + 48 * pair
            for i in range(CHUNKS):
                both = jnp.concatenate([parts[0][i], parts[1][i]], axis=0)
                panel[start : start + 48, chunk(i)] = both.astype(bf16)
            lengths += [jnp.sum(square, axis=1, keepdims=True) for square in squares]
    square = jnp.zeros((LASTS, LANES), f32)
    which = iota((LASTS, LANES), 0)
    for i in range(CHUNKS):
        piece = jnp.zeros((LASTS, LANES), f32)
        for half in range(2):
            for z in range(ZS):
                row = ends[half * ZS + z][i : i + 1]
                piece = jnp.where(which == last_row(half, z), row, piece)
        square = square + piece * piece
        panel[2 * MAIN :, chunk(i)] = piece.astype(bf16)
    lengths.append(jnp.sum(square, axis=1, keepdims=True))
    lengths = jnp.concatenate(lengths, axis=0) * (1.0 / temper)

    starts = [(0, 48), (MAIN, 48), (2 * MAIN, 8)]
    real = iota((8, 1), 0) < 4
    totals = [[jnp.zeros((rows, LANES), f32) for _ in range(CL_GRP)] for _, rows in starts]
    for j in range(ITEMS // STEP):
        columns = slice(j * STEP, (j + 1) * STEP)
        product = lax.dot_general(
            panel[...], items[columns, :], (((1,), (1,)), ((), ())), preferred_element_type=f32
        )
        logits = product * (2.0 / temper) - lengths
        tag = tags[:, columns]
        picked = []
        for start, rows in starts:
            chosen = logits[start : start + rows]
            for c in range(1, CL_GRP):
                chosen = jnp.where(tag == c, logits[start + c * rows : start + (c + 1) * rows], chosen)
            picked.append(chosen)
        picked[2] = jnp.where(real, picked[2], -3e38)
        highest = functools.reduce(jnp.maximum, [jnp.max(p, axis=0, keepdims=True) for p in picked])
        exponent = [jnp.exp(p - highest) for p in picked]
        scale = 1.0 / sum(jnp.sum(e, axis=0, keepdims=True) for e in exponent)
        for n, (start, rows) in enumerate(starts):
            weight = exponent[n] * scale
            owned = [jnp.where(tag == c, weight, 0.0) for c in range(CL_GRP)]
            for c in range(CL_GRP):
                for i in range(STEP // LANES):
                    totals[n][c] = totals[n][c] + owned[c][:, chunk(i)]
            if rows % 16:
                owned = [jnp.concatenate(owned[c : c + 2], axis=0) for c in range(0, CL_GRP, 2)]
            for c, part in enumerate(owned):
                size = part.shape[0]
                weights[start + c * size : start + (c + 1) * size, columns] = part.astype(bf16)

    for c in range(CL_GRP):
        marks[c, :48, :] = totals[0][c]
        marks[c, 48:, :] = totals[2][c]
    sums[...] = jnp.dot(weights[MAIN:, :], items[...], preferred_element_type=f32)
    pack_sums(send, sums, sums.at[MAIN:], total_rows(totals[1], totals[2], 1), 1)


def sweep(core, passages, blocks, first):
    out_shape = [
        jax.ShapeDtypeStruct((ZS, PACK, LANES), f32),
        jax.ShapeDtypeStruct((PANEL, ITEMS), bf16),
        jax.ShapeDtypeStruct((CL_GRP, 56, LANES), f32),
    ]
    if first:
        out_shape.append(jax.ShapeDtypeStruct((ITEMS, CHUNKS * LANES), bf16))
        out_shape.append(jax.ShapeDtypeStruct((1, ITEMS), f32))
    return pl.pallas_call(
        functools.partial(sweep_kernel, first),
        out_shape=out_shape,
        in_specs=[SCALARS] + [ON_CHIP] * (len(passages) + 1),
        out_specs=[ON_CHIP] * len(out_shape),
        scratch_shapes=[
            pltpu.VMEM((PANEL, CHUNKS * LANES), bf16),
            pltpu.VMEM((MAIN + LASTS, CHUNKS * LANES), f32),
        ],
        compiler_params=pltpu.CompilerParams(vmem_limit_bytes=32 * 2**20),
        name="sweep",
    )(core, *passages, blocks)


def kept_kernel(weights, items, marks, keep, sums, lasts):
    sums[...] = jnp.dot(weights[:MAIN, :], items[...], preferred_element_type=f32)
    lasts[...] = jnp.dot(weights[2 * MAIN :, :], items[...], preferred_element_type=f32)
    main = [marks[c, :48, :] for c in range(CL_GRP)]
    last = [marks[c, 48:, :] for c in range(CL_GRP)]
    pack_sums(keep, sums, lasts, total_rows(main, last, 0), 0)


def kept(weights, items, marks):
    features = CHUNKS * LANES
    return pl.pallas_call(
        kept_kernel,
        out_shape=jax.ShapeDtypeStruct((ZS, PACK, LANES), f32),
        in_specs=[ON_CHIP] * 3,
        out_specs=ON_CHIP,
        scratch_shapes=[pltpu.VMEM((MAIN, features), f32), pltpu.VMEM((LASTS, features), f32)],
        cost_estimate=pl.CostEstimate(
            flops=2 * (MAIN + LASTS) * ITEMS * features, bytes_accessed=4 * 2**20, transcendentals=0
        ),
        compiler_params=pltpu.CompilerParams(vmem_limit_bytes=16 * 2**20),
        name="kept",
    )(weights, items, marks)


def join_kernel(keep, received, out):
    which = iota((8, LANES), 0)
    for z in range(ZS):
        out[z, :144, :] = (keep[z, :144, :] + received[z, :144, :]).astype(bf16)
        end = keep[z, 144:152, :] + received[z, 144:152, :]
        rest = end - end.astype(bf16).astype(f32)
        end = jnp.where(which == 7, rest[6:7], end)
        out[z, 144:, :] = end.astype(bf16)


def join(keep, received):
    return pl.pallas_call(
        join_kernel,
        out_shape=jax.ShapeDtypeStruct((ZS, PACK, LANES), bf16),
        in_specs=[ON_CHIP] * 2,
        out_specs=ON_CHIP,
        compiler_params=pltpu.CompilerParams(vmem_limit_bytes=8 * 2**20),
        name="join",
    )(keep, received)


def update_kernel(parts, prior, out, *packed):
    total = parts[0].astype(f32)
    for z in range(1, ZS):
        total = total + parts[z].astype(f32)
    end = total[144:152]
    weight = to_column(end[6:7] + end[7:8], BLOCK) + 1.0
    before = prior[...].astype(f32)
    pieces, lasts = [], []
    for i in range(CHUNKS):
        piece = (total[24 * i : 24 * i + 24] + before[:24, chunk(i)]) / weight[:24]
        last = (end[i : i + 1] + before[24:25, chunk(i)]) / weight[24:25]
        out[:24, chunk(i)] = piece
        out[24:25, chunk(i)] = last
        pieces.append(piece)
        lasts.append(last)
    if packed:
        parts, end = pack_rows(pieces, lasts)
        for q in range(CHUNKS // 2):
            packed[0][0, 48 * q : 48 * q + 48, :] = parts[q].astype(bf16)
        packed[0][0, 144:, :] = end.astype(bf16)


def update(parts, prior, last):
    out_shape = [jax.ShapeDtypeStruct((OWN, CHUNKS * LANES), f32)]
    if not last:
        out_shape.append(jax.ShapeDtypeStruct((1, PACK, LANES), bf16))
    return pl.pallas_call(
        update_kernel,
        out_shape=out_shape,
        in_specs=[ON_CHIP] * 2,
        out_specs=[ON_CHIP] * len(out_shape),
        compiler_params=pltpu.CompilerParams(vmem_limit_bytes=8 * 2**20),
        name="update",
    )(parts, prior)


def shards(passages, labels, send_counts, send_offsets, owner_slot, centroids):
    members = lax.axis_size("member")
    along_z = [[m for m in range(members) if m % 2 == core] for core in range(2)]
    cores = [(m, m ^ 1) for m in range(members)]
    me = lax.axis_index("group").reshape(1).astype(jnp.int32)
    core = jnp.bitwise_and(lax.axis_index("member"), 1).reshape(1).astype(jnp.int32)

    outgoing = front(me, send_counts, send_offsets, labels, owner_slot, passages)
    passage_refs = [lax.all_to_all(outgoing, "group", split_axis=0, concat_axis=0, tiled=True)]
    packed = pack(centroids)
    prior = centroids
    for turn in range(ITERS):
        blocks = lax.all_gather(packed, "member", axis=0, tiled=True)
        send, weights, marks, *unpacked = sweep(core, passage_refs, blocks, turn == 0)
        passage_refs = unpacked or passage_refs
        received = lax.ppermute(send, "member", cores)
        keep = kept(weights, passage_refs[0], marks)
        parts = lax.all_to_all(
            join(keep, received), "member", split_axis=0, concat_axis=0, tiled=True, axis_index_groups=along_z
        )
        prior, *packed = update(parts, prior, turn == ITERS - 1)
        packed = packed[0] if packed else None
    return prior


def solution(mesh):
    spec = P(("group", "member"))
    rows = P(("group", "member"), None)
    return jax.shard_map(
        shards,
        mesh=mesh,
        in_specs=(rows, spec, rows, rows, P(), rows),
        out_specs=rows,
        check_vma=False,
    )
```
